32 devices in a mesh: head: 4 (over y, x), seq: 8 (over z, core).
Axes of the slice: x: 2, y: 2, z: 4, core: 2. Of those that a mesh axis runs over, the one named last changes fastest.
Arguments:
- tile_features: bfloat16 [8, 4, 512, 768], P('seq', 'head'), may hold values from -6 to 6
- slide_lengths: int32 [2], replicated, may hold values from 1025 to 10240, as said below
- qkv_weight: bfloat16 [768, 3, 768], P(None, None, 'head'), may hold values from -0.21875 to 0.21875
- qv_bias: float32 [2, 768], P(None, 'head'), may hold values from -2 to 2
- out_weight: bfloat16 [768, 768], P('head'), may hold values from -6 to 6
- out_bias: float32 [768], replicated, may hold values from -3 to 3
- attn_gain: float32 [768], replicated, may hold values from 0.5 to 1.5
- attn_shift: float32 [768], replicated, may hold values from -0.08 to 0.08
- mlp_gain: float32 [768], replicated, may hold values from 0.5 to 1.5
- mlp_shift: float32 [768], replicated, may hold values from -2 to 2
- up_weight: bfloat16 [768, 3072], P(None, 'head'), may hold values from -0.21875 to 0.21875
- up_bias: float32 [3072], P('head'), may hold values from -3 to 3
- down_weight: bfloat16 [3072, 768], P('head'), may hold values from -0.109375 to 0.109375
- down_bias: float32 [768], replicated, may hold values from -3 to 3
- output_cotangent: bfloat16 [8, 4, 512, 768], P('seq', 'head'), may hold values from -6 to 6
Outputs:
- output: bfloat16 [8, 4, 512, 768], P('seq', 'head')
- grad_features: float32 [8, 4, 512, 768], P('seq', 'head')
- grad_qkv_weight: float32 [768, 3, 768], P(None, None, 'head')
- grad_qv_bias: float32 [2, 768], P(None, 'head')
- grad_out_weight: float32 [768, 768], P('head')
- grad_out_bias: float32 [768], replicated
- grad_attn_gain: float32 [768], replicated
- grad_attn_shift: float32 [768], replicated
- grad_mlp_gain: float32 [768], replicated
- grad_mlp_shift: float32 [768], replicated
- grad_up_weight: float32 [768, 3072], P(None, 'head')
- grad_up_bias: float32 [3072], P('head')
- grad_down_weight: float32 [3072, 768], P('head')
- grad_down_bias: float32 [768], replicated
The draws below stay inside these ranges and needn't reach their ends.
Inputs may be any that keep to these rules, and one draw needn't show every extreme that they name: Slide k holds slide_lengths[k] valid tiles followed by padding up to a whole number of 1024-tile blocks, two or more; the slides lie one after another from tile 0 and fill all 16384 tiles exactly.
All inputs are finite; a program needn't handle non-finite values.
Results may differ from the reference program's by a relative error of at most 0.02.
Values may be sent and summed in bfloat16 or wider, within the bound.
A program may use at most 256 MiB of HBM per device.

```python
import jax
import jax.numpy as jnp
from jax import lax

D = 768
HEADS = 16
HEAD_WIDTH = 48
FF = 3072
SEGMENT_TILES = 1024
ROWS = 512
TOKENS = 16384
SLIDES = 2
N_HEAD = 4
N_SEQ = 8


def draw_slide_lengths(key, part):
    blocks_all = TOKENS // SEGMENT_TILES
    spare = blocks_all - 2 * SLIDES
    leader_extra = spare // 2 + SLIDES
    rest = spare - leader_extra
    key_scores, key_tails, key_lead = jax.random.split(jax.random.fold_in(key, 17), 3)
    leader = jax.random.randint(key_lead, (), 0, SLIDES).astype(jnp.int32)
    labels = jnp.arange(SLIDES, dtype=jnp.int32)
    is_leader = labels == leader
    root = jax.random.randint(key_scores, (SLIDES,), 1, 33).astype(jnp.int32)
    scores = jnp.where(is_leader, 0, root * root * root).astype(jnp.int32)
    share = (rest * scores // jnp.maximum(jnp.sum(scores), 1).astype(jnp.int32)).astype(jnp.int32)
    leftover = (rest - jnp.sum(share)).astype(jnp.int32)
    follower = ((leader + 1) % SLIDES).astype(jnp.int32)
    blocks = 2 + share + jnp.where(labels == follower, leftover, 0)
    blocks = jnp.where(is_leader, 2 + leader_extra, blocks).astype(jnp.int32)
    tails = jax.random.randint(key_tails, (SLIDES,), 1, SEGMENT_TILES + 1).astype(jnp.int32)
    tails = jnp.where(is_leader, SEGMENT_TILES, tails).astype(jnp.int32)
    return ((blocks - 1) * SEGMENT_TILES + tails).astype(jnp.int32)


def draw_qv_bias(key, part):
    key = jax.random.fold_in(key, 29)
    row_scale = jnp.array([0.5, 0.02], jnp.float32)[:, None]
    base = jnp.clip(jax.random.normal(key, (2, D), jnp.float32), -4.0, 4.0)
    return base * row_scale


def steps_of(own_key, extent, shards, smallest, high):
    def one(axis_at, parts):
        steps = jax.random.uniform(jax.random.fold_in(jax.random.fold_in(own_key, 6), axis_at), (parts,), jnp.float32, smallest / len(shards), high / len(shards))
        return jnp.repeat(jnp.exp(steps), extent[axis_at] // parts).reshape((-1,) + (1,) * (len(extent) - axis_at - 1))

    gain = one(*shards[0])
    for cut in shards[1:]:
        gain = gain * one(*cut)
    return gain


def normal_values(rng, shape, width, reach, shards=(), kind=jnp.bfloat16):
    values = width * jax.random.normal(rng, shape, jnp.float32)
    if shards:
        values = values * steps_of(rng, shape, shards, -0.22, 0.18)
    return jnp.clip(values, -reach, reach).astype(kind)


def setup_inputs(seed: int = 0) -> dict:
    arg_keys = jax.random.split(jax.random.key(seed), 16)
    tile_features = normal_values(arg_keys[0], (N_SEQ, N_HEAD, ROWS, D), 1.0, 6.0, ((0, 8), (1, 4)))
    slide_lengths = draw_slide_lengths(jax.random.fold_in(arg_keys[15], 71), 0)
    qkv_weight = normal_values(arg_keys[2], (D, 3, D), D ** -0.5, 0.21875, ((2, 4),))
    qv_bias = draw_qv_bias(jax.random.fold_in(arg_keys[15], 71), 0)
    out_weight = normal_values(arg_keys[4], (D, D), 1 ** -0.5, 6.0, ((0, 4),))
    out_bias = normal_values(arg_keys[5], (D,), 0.5, 3.0, (), jnp.float32)
    attn_gain = jnp.clip(1.0 + 0.1 * jax.random.normal(arg_keys[6], (D,), jnp.float32), 0.5, 1.5)
    attn_shift = normal_values(arg_keys[7], (D,), 0.03, 0.08, (), jnp.float32)
    mlp_gain = jnp.clip(1.0 + 0.1 * jax.random.normal(arg_keys[8], (D,), jnp.float32), 0.5, 1.5)
    mlp_shift = normal_values(arg_keys[9], (D,), 0.3, 2.0, (), jnp.float32)
    up_weight = normal_values(arg_keys[10], (D, FF), D ** -0.5, 0.21875, ((1, 4),))
    up_bias = normal_values(arg_keys[11], (FF,), 0.5, 3.0, ((0, 4),), jnp.float32)
    down_weight = normal_values(arg_keys[12], (FF, D), FF ** -0.5, 0.109375, ((0, 4),))
    down_bias = normal_values(arg_keys[13], (D,), 0.5, 3.0, (), jnp.float32)
    output_cotangent = normal_values(arg_keys[14], (N_SEQ, N_HEAD, ROWS, D), 1.0, 6.0, ((0, 8), (1, 4)))
    return {"tile_features": tile_features, "slide_lengths": slide_lengths, "qkv_weight": qkv_weight, "qv_bias": qv_bias, "out_weight": out_weight, "out_bias": out_bias, "attn_gain": attn_gain, "attn_shift": attn_shift, "mlp_gain": mlp_gain, "mlp_shift": mlp_shift, "up_weight": up_weight, "up_bias": up_bias, "down_weight": down_weight, "down_bias": down_bias, "output_cotangent": output_cotangent}


@jax.custom_vjp
def low(v):
    return lax.optimization_barrier(v.astype(jnp.bfloat16)).astype(jnp.float32)

@jax.custom_vjp
def low_back(v):
    return v

def low_keep(v):
    return (low(v), None)

def low_pass(kept, grad):
    return (grad,)

def back_keep(v):
    return (v, None)

def back_low(kept, grad):
    return (low(grad),)
low.defvjp(low_keep, low_pass)
low_back.defvjp(back_keep, back_low)
epsilon = 1e-05
masked_low = -1e+30
highest = lax.Precision.HIGHEST

def layout(slide_lengths, positions):
    blocks = (slide_lengths + SEGMENT_TILES - 1) // SEGMENT_TILES
    slide_ends = (jnp.cumsum(blocks) * SEGMENT_TILES).astype(jnp.int32)
    slide_starts = (slide_ends - blocks * SEGMENT_TILES).astype(jnp.int32)
    inside = (positions[..., None] >= slide_starts) & (positions[..., None] < slide_ends)
    labels = jnp.arange(slide_lengths.shape[0], dtype=jnp.int32)
    slide_index = lax.optimization_barrier(jnp.sum(jnp.where(inside, labels, 0), axis=-1)).astype(jnp.int32)
    offset = (positions - lax.optimization_barrier(jnp.sum(jnp.where(inside, slide_starts, 0), axis=-1))).astype(jnp.int32)
    length = lax.optimization_barrier(jnp.sum(jnp.where(inside, slide_lengths, 0), axis=-1)).astype(jnp.int32)
    return (slide_index, offset < length)

def norm_apply(values, norm_gain, norm_shift):
    center = values - lax.optimization_barrier(jnp.mean(values, axis=-1, keepdims=True))
    variance = lax.optimization_barrier(jnp.mean(center * center, axis=-1, keepdims=True))
    return center * lax.rsqrt(variance + epsilon) * norm_gain + norm_shift

def level_head(query_rows, key_rows, value_rows, slide_all, valid_all, phase, dilation_step, score_scale):
    count_blocks = TOKENS // (SEGMENT_TILES * dilation_step)

    def pick_phase(source):
        folded = source.reshape((TOKENS // dilation_step, dilation_step) + source.shape[1:])[:, phase]
        return folded.reshape((count_blocks, SEGMENT_TILES) + source.shape[1:])

    def one_block(block_args):
        query_block, key_block, value_block, slide_block, valid_block = block_args
        allowed = (slide_block[:, None] == slide_block[None, :]) & valid_block[None, :]
        scores = low_back(jnp.dot(query_block, key_block.T, precision=highest) * score_scale)
        masked = jnp.where(allowed, scores, masked_low)
        row_maximum = lax.optimization_barrier(jnp.max(masked, axis=1))
        weights = jnp.where(allowed, jnp.exp(masked - row_maximum[:, None]), 0.0)
        return (row_maximum, lax.optimization_barrier(jnp.sum(weights, axis=1)), jnp.dot(low(weights), value_block, precision=highest))
    row_maximum, row_denominator, row_numerator = lax.map(jax.checkpoint(one_block), (pick_phase(query_rows), pick_phase(key_rows), pick_phase(value_rows), pick_phase(slide_all), pick_phase(valid_all)))

    def place_back(values, fill_value):
        flat = values.reshape((TOKENS // dilation_step,) + values.shape[2:])
        full = jnp.full((TOKENS // dilation_step, dilation_step) + values.shape[2:], fill_value, jnp.float32)
        return full.at[:, phase].set(flat).reshape((TOKENS,) + values.shape[2:])
    return (place_back(row_maximum, masked_low), place_back(row_denominator, 0.0), place_back(row_numerator, 0.0))

def reference(tile_features, slide_lengths, qkv_weight, qv_bias, out_weight, out_bias, attn_gain, attn_shift, mlp_gain, mlp_shift, up_weight, up_bias, down_weight, down_bias, output_cotangent):
    positions = jnp.arange(TOKENS, dtype=jnp.int32)
    slide_all, valid_all = layout(slide_lengths, positions)
    score_scale = HEAD_WIDTH ** (-0.5)

    def forward(features, qkv_w, qv_b, out_w, out_b, a_gain, a_shift, m_gain, m_shift, up_w, up_b, down_w, down_b):
        normed_one = low(norm_apply(features, a_gain, a_shift))
        projected = jnp.dot(normed_one, qkv_w.reshape(D, 3 * D), precision=highest).reshape(TOKENS, 3, D)
        bias_full = jnp.stack([qv_b[0], jnp.zeros((D,), jnp.float32), qv_b[1]])
        projected = low(low_back(projected + bias_full))
        heads_out = []
        for head_index in range(HEADS):
            columns = slice(head_index * HEAD_WIDTH, (head_index + 1) * HEAD_WIDTH)
            query_rows = projected[:, 0, columns]
            key_rows = projected[:, 1, columns]
            value_rows = projected[:, 2, columns]
            peaks, totals, numers = ([], [], [])
            for level_index in range(5):
                dilation_step = 2 ** level_index
                found = level_head(query_rows, key_rows, value_rows, slide_all, valid_all, head_index % dilation_step, dilation_step, score_scale)
                peaks.append(found[0])
                totals.append(found[1])
                numers.append(found[2])
            peaks = jnp.stack(peaks)
            best_peak = lax.optimization_barrier(jnp.max(peaks, axis=0))
            factor = jnp.exp(peaks - best_peak)
            denom_all = lax.optimization_barrier(jnp.sum(factor * jnp.stack(totals), axis=0))
            heads_out.append(lax.optimization_barrier(jnp.sum(factor[..., None] * jnp.stack(numers), axis=0)) / denom_all[:, None])
        attention = jnp.concatenate(heads_out, axis=1)
        attn_low = low(low_back(attention))
        residual = features + low_back(jnp.dot(attn_low, out_w, precision=highest)) + out_b

        def mlp_block(rows_in):
            normed_two = low(norm_apply(rows_in, m_gain, m_shift))
            pre_act = low_back(jnp.dot(normed_two, up_w, precision=highest) + up_b)
            hidden = low(jax.nn.gelu(pre_act, approximate=True))
            return rows_in + low_back(jnp.dot(hidden, down_w, precision=highest)) + down_b
        block_row_count = min(4096, TOKENS)
        result = lax.map(jax.checkpoint(mlp_block), residual.reshape(TOKENS // block_row_count, block_row_count, D))
        return result.reshape(TOKENS, D)
    inputs_f32 = (tile_features.reshape(TOKENS, D).astype(jnp.float32), qkv_weight.astype(jnp.float32), qv_bias, out_weight.astype(jnp.float32), out_bias, attn_gain, attn_shift, mlp_gain, mlp_shift, up_weight.astype(jnp.float32), up_bias, down_weight.astype(jnp.float32), down_bias)
    result, pullback = jax.vjp(forward, *inputs_f32)
    gradients = pullback(output_cotangent.reshape(TOKENS, D).astype(jnp.float32))
    output = result.astype(jnp.bfloat16).reshape(tile_features.shape)
    return (output, gradients[0].reshape(tile_features.shape), gradients[1], gradients[2], gradients[3], gradients[4], gradients[5], gradients[6], gradients[7], gradients[8], gradients[9], gradients[10], gradients[11], gradients[12])
```

```python
import functools
import math

import jax
import jax.numpy as jnp
import numpy as np
from jax import lax
from jax.experimental import pallas as pl
from jax.experimental.pallas import tpu as pltpu
from jax.sharding import PartitionSpec as P

HEAD_WIDTH = 48
SEGMENT_TILES = 1024
LEVELS = 5
RESIDUES = 16
LANES = 128
RING_KEYS = SEGMENT_TILES // 2
ORDER = (0, 8, 4, 12, 2, 6, 10, 14, 1, 3, 5, 7, 9, 11, 13, 15)
SLAB = SEGMENT_TILES // RESIDUES

epsilon = 1e-05
masked_low = -1e30
BF16 = jnp.bfloat16
F32 = jnp.float32
LN2 = math.log(2.0)
SUM_LANE = 2 * HEAD_WIDTH
AUX_LANE = SUM_LANE + 1
AUX_COUNT = 3
VMEM_LIMIT = 52 * 1024 * 1024


def dot(left_side, right_side, left_dim, right_dim):
    return lax.dot_general(
        left_side,
        right_side,
        (((left_dim,), (right_dim,)), ((), ())),
        preferred_element_type=F32,
    )


def class_rows(level):
    low = SEGMENT_TILES >> (level + 1) if level < LEVELS - 1 else 0
    return low, SEGMENT_TILES >> level


def key_class():
    index = np.arange(SEGMENT_TILES)
    found = np.zeros(SEGMENT_TILES, np.int64)
    for level in range(LEVELS):
        found[index < SEGMENT_TILES >> level] = level
    return found


def multiplicity_table():
    classes = key_class()
    table = np.zeros((LEVELS, SEGMENT_TILES + (LEVELS - 1) * RING_KEYS), np.float32)
    for level in range(LEVELS):
        table[level, :SEGMENT_TILES] = 1 + np.minimum(level, classes)
        for ring in range(1, level + 1):
            prefix = SEGMENT_TILES >> ring
            one = np.minimum(level, classes[:prefix]) - ring + 1
            start = SEGMENT_TILES + (ring - 1) * RING_KEYS
            table[level, start : start + RING_KEYS] = np.tile(one, RING_KEYS // prefix)
    return table


def layout(slide_lengths, positions):
    blocks = (slide_lengths + SEGMENT_TILES - 1) // SEGMENT_TILES
    slide_ends = jnp.cumsum(blocks) * SEGMENT_TILES
    slide_starts = slide_ends - blocks * SEGMENT_TILES
    inside = (positions[..., None] >= slide_starts) & (positions[..., None] < slide_ends)
    labels = jnp.arange(slide_lengths.shape[0], dtype=jnp.int32)
    slide_index = jnp.sum(jnp.where(inside, labels, 0), axis=-1)
    offset = positions - jnp.sum(jnp.where(inside, slide_starts, 0), axis=-1)
    length = jnp.sum(jnp.where(inside, slide_lengths, 0), axis=-1)
    return (slide_index, offset < length)


def ring_members(ring, block_count):
    return range((1 << (ring - 1)) // block_count, (1 << ring) // block_count)


def key_bias(slide_lengths, sequence_member, base_head, heads, block_count, row_count):
    local_rings = block_count.bit_length() - 1
    index = np.arange(SEGMENT_TILES)
    order = np.asarray(ORDER)[index // SLAB]
    piece = row_count // RESIDUES
    spot = (index % SLAB) // piece * row_count + index % piece * RESIDUES
    head = base_head + jnp.arange(heads, dtype=jnp.int32)[:, None]
    inner = spot[None, :] + (head + order[None, :]) % RESIDUES
    first_block = sequence_member * block_count
    per_block = []
    for block in range(block_count):
        parts = [(first_block + block) * SEGMENT_TILES + inner]
        for ring in range(1, LEVELS):
            prefix = SEGMENT_TILES >> ring
            if ring <= local_rings:
                start = (block >> (ring - 1) ^ 1) << (ring - 1)
                ids = [first_block + start + t for t in range(1 << (ring - 1))]
            else:
                ids = [
                    (sequence_member ^ x) * block_count + t
                    for x in ring_members(ring, block_count)
                    for t in range(block_count)
                ]
            parts += [one * SEGMENT_TILES + inner[:, :prefix] for one in ids]
        per_block.append(jnp.concatenate(parts, axis=1))
    positions = jnp.stack(per_block, axis=1).astype(jnp.int32)
    slide, valid = layout(slide_lengths, positions)
    own, _ = layout(
        slide_lengths,
        (first_block + jnp.arange(block_count, dtype=jnp.int32)) * SEGMENT_TILES,
    )
    allowed = (slide == own[None, :, None]) & valid
    table = multiplicity_table()
    logs = np.where(table > 0, np.log2(np.maximum(table, 1)), masked_low).astype(np.float32)
    return jnp.where(allowed[:, :, None, :], logs[None, None], masked_low)


def project_kernel(heads, row_count, base_ref, x_ref, w_ref, b_ref, q_ref, kv_ref, held_ref):
    piece = row_count // RESIDUES
    halves = SEGMENT_TILES // row_count
    for half in range(halves):
        x = x_ref[half * row_count : (half + 1) * row_count, :]
        for head in range(heads):
            columns = slice(head * 2 * LANES, (head + 1) * 2 * LANES)
            wide = dot(x, w_ref[:, columns], 1, 0) + b_ref[0:1, columns]
            held_ref[...] = (wide * b_ref[1:2, columns]).astype(BF16)
            for slab in range(RESIDUES):
                residue = lax.rem(base_ref[0] + head + ORDER[slab], RESIDUES)
                source = pl.ds(pl.multiple_of(residue * piece, piece), piece)
                start = slab * SLAB + half * piece
                q_ref[head, 0, start : start + piece, :] = held_ref[source, :LANES]
                kv_ref[head, 0, start : start + piece, :] = held_ref[source, LANES:]


def project(base, rows, weight, bias, heads, row_count):
    total, width = rows.shape
    blocks = total // SEGMENT_TILES
    shape = jax.ShapeDtypeStruct((heads, blocks, SEGMENT_TILES, LANES), BF16)
    spec = pl.BlockSpec((heads, 1, SEGMENT_TILES, LANES), lambda k, *_: (0, k, 0, 0))
    return pl.pallas_call(
        functools.partial(project_kernel, heads, row_count),
        grid_spec=pltpu.PrefetchScalarGridSpec(
            num_scalar_prefetch=1,
            grid=(blocks,),
            in_specs=[
                pl.BlockSpec((SEGMENT_TILES, width), lambda k, *_: (k, 0)),
                pl.BlockSpec(weight.shape, lambda k, *_: (0, 0)),
                pl.BlockSpec(bias.shape, lambda k, *_: (0, 0)),
            ],
            out_specs=[spec, spec],
            scratch_shapes=[pltpu.VMEM((row_count, 2 * LANES), BF16)],
        ),
        out_shape=[shape, shape],
        cost_estimate=pl.CostEstimate(
            flops=2 * total * width * weight.shape[1], bytes_accessed=8 * total * width, transcendentals=0
        ),
        compiler_params=pltpu.CompilerParams(vmem_limit_bytes=VMEM_LIMIT),
        name="project",
    )(base, rows, weight, bias)


def split_three(value):
    high = value.astype(BF16).astype(F32)
    rest = value - high
    middle = rest.astype(BF16).astype(F32)
    return high, middle, rest - middle


def with_aux(rows, value):
    lane = lax.broadcasted_iota(jnp.int32, rows.shape, 1)
    filled = rows.astype(F32)
    for step, part in enumerate(split_three(value)):
        filled = jnp.where(lane == AUX_LANE + step, part, filled)
    return filled.astype(BF16)


def finish(total, peak, q):
    denominator = total[:, SUM_LANE : SUM_LANE + 1]
    lse = peak + jnp.log(denominator) * (1.0 / LN2)
    return total / denominator, with_aux(q, -lse)


def local_pieces(kv_ref, block, ring):
    count = 1 << (ring - 1)
    start = (block // count) ^ 1
    prefix = SEGMENT_TILES >> ring
    return [(start * count + t, prefix) for t in range(count)]


def attend_near_kernel(local_rings, q_ref, kv_ref, bias_ref, o_ref, qa_ref):
    block = pl.program_id(1)
    first = SEGMENT_TILES >> (local_rings + 1)
    for level in range(local_rings + 1):
        low, high = class_rows(level)
        size = min(256, high - low)
        for start in range(low, high, size):
            q = q_ref[0, 0, start : start + size, :]
            keys = [(kv_ref[0, block], 0)]
            place = SEGMENT_TILES
            for ring in range(1, level + 1):
                for other, prefix in local_pieces(kv_ref, block, ring):
                    keys.append((kv_ref[0, other, :prefix], place))
                    place += prefix
            scores = [
                dot(q, kv, 1, 1) + bias_ref[0, 0, level : level + 1, at : at + kv.shape[0]]
                for kv, at in keys
            ]
            peak = functools.reduce(
                jnp.maximum, [jnp.max(s, axis=1, keepdims=True) for s in scores]
            )
            total = sum(
                dot(jnp.exp2(s - peak).astype(BF16), kv, 1, 0) for s, (kv, _) in zip(scores, keys)
            )
            out, extended = finish(total, peak, q)
            o_ref[0, 0, start - first : start - first + size, :] = out
            qa_ref[0, 0, start - first : start - first + size, :] = extended


def attend_near(q, kv, bias):
    heads, blocks = q.shape[:2]
    local_rings = blocks.bit_length() - 1
    rows = SEGMENT_TILES - (SEGMENT_TILES >> (local_rings + 1))
    spec = pl.BlockSpec((1, 1, rows, LANES), lambda h, k: (h, k, 0, 0))
    pairs = heads * blocks * rows * 1400
    return pl.pallas_call(
        functools.partial(attend_near_kernel, local_rings),
        grid=(heads, blocks),
        in_specs=[
            pl.BlockSpec((1, 1, SEGMENT_TILES, LANES), lambda h, k: (h, k, 0, 0)),
            pl.BlockSpec((1, blocks, SEGMENT_TILES, LANES), lambda h, k: (h, 0, 0, 0)),
            pl.BlockSpec((1, 1) + bias.shape[2:], lambda h, k: (h, k, 0, 0)),
        ],
        out_specs=[spec, spec],
        out_shape=[
            jax.ShapeDtypeStruct((heads, blocks, rows, LANES), F32),
            jax.ShapeDtypeStruct((heads, blocks, rows, LANES), BF16),
        ],
        cost_estimate=pl.CostEstimate(
            flops=pairs * 1024, bytes_accessed=heads * blocks * rows * 1500, transcendentals=pairs
        ),
        compiler_params=pltpu.CompilerParams(vmem_limit_bytes=VMEM_LIMIT),
        name="attend_near",
    )(q, kv, bias)


def far_groups(local_rings):
    groups = []
    for level in range(local_rings + 1, LEVELS):
        low, high = class_rows(level)
        groups.append((level, low, high))
    return sorted(groups, key=lambda group: group[1])


def add_bias(scores, bias_ref, block, at, groups, rows):
    width = scores.shape[1]
    parts = []
    for level, low, high in groups:
        if low < rows:
            parts.append(scores[low:high] + bias_ref[0, block, level : level + 1, at : at + width])
    return parts[0] if len(parts) == 1 else jnp.concatenate(parts, axis=0)


def far_score_list(local_rings, blocks, left_ref, kv_ref, far_ref):
    rows = SEGMENT_TILES >> (local_rings + 1)
    pieces = []
    for block in range(blocks):
        pieces.append((0, block, block, SEGMENT_TILES, rows, 0))
    for block in range(blocks):
        place = SEGMENT_TILES
        for ring in range(1, local_rings + 1):
            for other, prefix in local_pieces(kv_ref, block, ring):
                pieces.append((ring, block, other, prefix, rows, place))
                place += prefix
    for ring in range(local_rings + 1, LEVELS):
        pieces.append((ring, None, None, RING_KEYS, SEGMENT_TILES >> ring, SEGMENT_TILES + (ring - 1) * RING_KEYS))
    return pieces


def far_keys(piece, kv_ref, far_ref, local_rings):
    ring, block, other, prefix, rows, place = piece
    if block is not None:
        return kv_ref[0, other, :prefix]
    start = (ring - local_rings - 1) * RING_KEYS
    return far_ref[0, start : start + RING_KEYS, :]


def far_left(piece, left_ref, blocks):
    ring, block, other, prefix, rows, place = piece
    if block is not None:
        return left_ref[0, block, :rows, :]
    return jnp.concatenate([left_ref[0, one, :rows, :] for one in range(blocks)], axis=0)


def pad_rows(value, rows, fill):
    if value.shape[0] == rows:
        return value
    return jnp.concatenate(
        [value, jnp.full((rows - value.shape[0],) + value.shape[1:], fill, value.dtype)], axis=0
    )


def attend_far_kernel(local_rings, blocks, q_ref, kv_ref, far_ref, bias_ref, o_ref, qa_ref):
    rows = SEGMENT_TILES >> (local_rings + 1)
    groups = far_groups(local_rings)
    pieces = far_score_list(local_rings, blocks, q_ref, kv_ref, far_ref)
    held = []
    peaks = [None] * blocks
    for piece in pieces:
        ring, block, other, prefix, count, place = piece
        scores = dot(far_left(piece, q_ref, blocks), far_keys(piece, kv_ref, far_ref, local_rings), 1, 1)
        for one in [block] if block is not None else range(blocks):
            part = scores if block is not None else scores[one * count : (one + 1) * count]
            part = add_bias(part, bias_ref, one, place, groups, count)
            held.append((piece, one, part))
            top = pad_rows(jnp.max(part, axis=1, keepdims=True), rows, masked_low)
            peaks[one] = top if peaks[one] is None else jnp.maximum(peaks[one], top)
    totals = [jnp.zeros((rows, LANES), F32)] * blocks
    for piece in pieces:
        weights = [
            (one, jnp.exp2(part - peaks[one][: piece[4]]).astype(BF16))
            for owner, one, part in held
            if owner is piece
        ]
        joined = weights[0][1] if len(weights) == 1 else jnp.concatenate([w for _, w in weights], axis=0)
        product = dot(joined, far_keys(piece, kv_ref, far_ref, local_rings), 1, 0)
        for at, (one, _) in enumerate(weights):
            part = product[at * piece[4] : (at + 1) * piece[4]]
            totals[one] = totals[one] + pad_rows(part, rows, 0.0)
    for block in range(blocks):
        out, extended = finish(totals[block], peaks[block], q_ref[0, block, :rows, :])
        o_ref[0, block] = out
        qa_ref[0, block] = extended


def attend_far(q, kv, far, bias):
    heads, blocks = q.shape[:2]
    local_rings = blocks.bit_length() - 1
    rows = SEGMENT_TILES >> (local_rings + 1)
    whole = lambda shape: pl.BlockSpec((1,) + shape[1:], lambda h: (h,) + (0,) * (len(shape) - 1))
    shape = (heads, blocks, rows, LANES)
    pairs = heads * blocks * rows * 2600
    return pl.pallas_call(
        functools.partial(attend_far_kernel, local_rings, blocks),
        grid=(heads,),
        in_specs=[
            pl.BlockSpec((1, blocks, rows, LANES), lambda h: (h, 0, 0, 0)),
            whole(kv.shape),
            whole(far.shape),
            whole(bias.shape),
        ],
        out_specs=[whole(shape), whole(shape)],
        out_shape=[jax.ShapeDtypeStruct(shape, F32), jax.ShapeDtypeStruct(shape, BF16)],
        cost_estimate=pl.CostEstimate(
            flops=pairs * 1024, bytes_accessed=heads * 4 * 1024 * 1024, transcendentals=pairs
        ),
        compiler_params=pltpu.CompilerParams(vmem_limit_bytes=VMEM_LIMIT),
        name="attend_far",
    )(q, kv, far, bias)


def placement(heads):
    table = np.zeros((heads * LANES, heads * HEAD_WIDTH), np.float32)
    for head in range(heads):
        for column in range(HEAD_WIDTH):
            table[head * LANES + HEAD_WIDTH + column, head * HEAD_WIDTH + column] = 1
    return table


def pack_kernel(heads, row_count, base_ref, far_ref, near_ref, place_ref, out_ref, held_ref):
    piece = row_count // RESIDUES
    halves = SEGMENT_TILES // row_count
    far_rows = far_ref.shape[2]
    for head in range(heads):
        columns = slice(head * LANES, (head + 1) * LANES)
        for slab in range(RESIDUES):
            residue = lax.rem(base_ref[0] + head + ORDER[slab], RESIDUES)
            for half in range(halves):
                start = slab * SLAB + half * piece
                if start < far_rows:
                    value = far_ref[head, 0, start : start + piece, :]
                else:
                    value = near_ref[head, 0, start - far_rows : start - far_rows + piece, :]
                target = pl.ds(pl.multiple_of(half * row_count + residue * piece, piece), piece)
                held_ref[target, columns] = value.astype(BF16)
    out_ref[...] = dot(held_ref[...], place_ref[...], 1, 0).astype(BF16)


def pack(base, far, near, row_count):
    heads, blocks = far.shape[:2]
    place = jnp.asarray(placement(heads), BF16)
    width = heads * HEAD_WIDTH
    part = lambda shape: pl.BlockSpec((heads, 1) + shape[2:], lambda k, *_: (0, k, 0, 0))
    return pl.pallas_call(
        functools.partial(pack_kernel, heads, row_count),
        grid_spec=pltpu.PrefetchScalarGridSpec(
            num_scalar_prefetch=1,
            grid=(blocks,),
            in_specs=[part(far.shape), part(near.shape), pl.BlockSpec(place.shape, lambda k, *_: (0, 0))],
            out_specs=pl.BlockSpec((SEGMENT_TILES, width), lambda k, *_: (k, 0)),
            scratch_shapes=[pltpu.VMEM((SEGMENT_TILES, heads * LANES), BF16)],
        ),
        out_shape=jax.ShapeDtypeStruct((blocks * SEGMENT_TILES, width), BF16),
        cost_estimate=pl.CostEstimate(
            flops=2 * blocks * SEGMENT_TILES * heads * LANES * width,
            bytes_accessed=blocks * SEGMENT_TILES * heads * LANES * 5,
            transcendentals=0,
        ),
        compiler_params=pltpu.CompilerParams(vmem_limit_bytes=VMEM_LIMIT),
        name="pack",
    )(base, far, near, place)


def unpack_kernel(heads, row_count, base_ref, g_ref, far_ref, near_ref, place_ref, out_ref, held_ref):
    piece = row_count // RESIDUES
    halves = SEGMENT_TILES // row_count
    far_rows = far_ref.shape[2]
    held_ref[...] = dot(g_ref[...], place_ref[...], 1, 1)
    for head in range(heads):
        columns = slice(head * LANES, (head + 1) * LANES)
        for slab in range(RESIDUES):
            residue = lax.rem(base_ref[0] + head + ORDER[slab], RESIDUES)
            for half in range(halves):
                start = slab * SLAB + half * piece
                if start < far_rows:
                    value = far_ref[head, 0, start : start + piece, :]
                else:
                    value = near_ref[head, 0, start - far_rows : start - far_rows + piece, :]
                source = pl.ds(pl.multiple_of(half * row_count + residue * piece, piece), piece)
                grad = held_ref[source, columns]
                delta = jnp.sum(grad * value, axis=1, keepdims=True)
                out_ref[head, 0, start : start + piece, :] = with_aux(grad, -delta)


def unpack(base, grad, far, near, row_count):
    heads, blocks = far.shape[:2]
    place = jnp.asarray(placement(heads), BF16)
    width = heads * HEAD_WIDTH
    part = lambda shape: pl.BlockSpec((heads, 1) + shape[2:], lambda k, *_: (0, k, 0, 0))
    shape = (heads, blocks, SEGMENT_TILES, LANES)
    return pl.pallas_call(
        functools.partial(unpack_kernel, heads, row_count),
        grid_spec=pltpu.PrefetchScalarGridSpec(
            num_scalar_prefetch=1,
            grid=(blocks,),
            in_specs=[
                pl.BlockSpec((SEGMENT_TILES, width), lambda k, *_: (k, 0)),
                part(far.shape),
                part(near.shape),
                pl.BlockSpec(place.shape, lambda k, *_: (0, 0)),
            ],
            out_specs=part(shape),
            scratch_shapes=[pltpu.VMEM((SEGMENT_TILES, heads * LANES), F32)],
        ),
        out_shape=jax.ShapeDtypeStruct(shape, BF16),
        cost_estimate=pl.CostEstimate(
            flops=2 * blocks * SEGMENT_TILES * heads * LANES * width,
            bytes_accessed=blocks * SEGMENT_TILES * heads * LANES * 7,
            transcendentals=0,
        ),
        compiler_params=pltpu.CompilerParams(vmem_limit_bytes=VMEM_LIMIT),
        name="unpack",
    )(base, grad, far, near, place)


def back_near_kernel(local_rings, qa_ref, do_ref, kv_ref, bias_ref, dq_ref, dkv_ref):
    block = pl.program_id(1)
    first = SEGMENT_TILES >> (local_rings + 1)

    @pl.when(block == 0)
    def _():
        dkv_ref[...] = jnp.zeros_like(dkv_ref)

    for level in range(local_rings + 1):
        low, high = class_rows(level)
        size = min(256, high - low)
        for start in range(low, high, size):
            here = slice(start - first, start - first + size)
            q = qa_ref[0, 0, here, :]
            grad = do_ref[0, 0, start : start + size, :]
            q_turned, grad_turned = q.T, grad.T
            keys = [(block, SEGMENT_TILES, 0)]
            place = SEGMENT_TILES
            for ring in range(1, level + 1):
                for other, prefix in local_pieces(kv_ref, block, ring):
                    keys.append((other, prefix, place))
                    place += prefix
            dq = jnp.zeros((size, LANES), F32)
            for other, prefix, at in keys:
                kv = kv_ref[0, other, :prefix]
                scores = dot(q, kv, 1, 1) + bias_ref[0, 0, level : level + 1, at : at + prefix]
                weights = jnp.exp2(scores)
                grads = (weights * dot(grad, kv, 1, 1)).astype(BF16)
                dq = dq + dot(grads, kv, 1, 0)
                dkv_ref[0, other, :, :prefix] += dot(q_turned, grads, 1, 0) + dot(
                    grad_turned, weights.astype(BF16), 1, 0
                )
            dq_ref[0, 0, here, :] = dq


def back_near(qa, do, kv, bias):
    heads, blocks = kv.shape[:2]
    local_rings = blocks.bit_length() - 1
    rows = qa.shape[2]
    spec = pl.BlockSpec((1, 1, rows, LANES), lambda h, k: (h, k, 0, 0))
    pairs = heads * blocks * rows * 1400
    return pl.pallas_call(
        functools.partial(back_near_kernel, local_rings),
        grid=(heads, blocks),
        in_specs=[
            spec,
            pl.BlockSpec((1, 1, SEGMENT_TILES, LANES), lambda h, k: (h, k, 0, 0)),
            pl.BlockSpec((1, blocks, SEGMENT_TILES, LANES), lambda h, k: (h, 0, 0, 0)),
            pl.BlockSpec((1, 1) + bias.shape[2:], lambda h, k: (h, k, 0, 0)),
        ],
        out_specs=[spec, pl.BlockSpec((1, blocks, LANES, SEGMENT_TILES), lambda h, k: (h, 0, 0, 0))],
        out_shape=[
            jax.ShapeDtypeStruct((heads, blocks, rows, LANES), F32),
            jax.ShapeDtypeStruct((heads, blocks, LANES, SEGMENT_TILES), F32),
        ],
        cost_estimate=pl.CostEstimate(
            flops=pairs * 2560, bytes_accessed=heads * blocks * rows * 2500, transcendentals=pairs
        ),
        compiler_params=pltpu.CompilerParams(vmem_limit_bytes=VMEM_LIMIT),
        name="back_near",
    )(qa, do, kv, bias)


def back_far_kernel(
    local_rings, blocks, qa_ref, do_ref, kv_ref, far_ref, bias_ref, dq_ref, dkv_ref, dfar_ref
):
    rows = SEGMENT_TILES >> (local_rings + 1)
    groups = far_groups(local_rings)
    dq_ref[...] = jnp.zeros_like(dq_ref)
    for piece in far_score_list(local_rings, blocks, qa_ref, kv_ref, far_ref):
        ring, block, other, prefix, count, place = piece
        q = far_left(piece, qa_ref, blocks)
        grad = far_left(piece, do_ref, blocks)
        kv = far_keys(piece, kv_ref, far_ref, local_rings)
        raw = dot(q, kv, 1, 1)
        owners = [block] if block is not None else range(blocks)
        parts = [
            add_bias(raw[at * count : (at + 1) * count], bias_ref, one, place, groups, count)
            for at, one in enumerate(owners)
        ]
        scores = parts[0] if len(parts) == 1 else jnp.concatenate(parts, axis=0)
        weights = jnp.exp2(scores)
        grads = (weights * dot(grad, kv, 1, 1)).astype(BF16)
        dq = dot(grads, kv, 1, 0)
        for at, one in enumerate(owners):
            dq_ref[0, one, :count, :] += dq[at * count : (at + 1) * count]
        dkv = dot(q.T, grads, 1, 0) + dot(grad.T, weights.astype(BF16), 1, 0)
        if block is None:
            start = (ring - local_rings - 1) * RING_KEYS
            dfar_ref[0, start : start + RING_KEYS, :] = dkv.T.astype(BF16)
        elif ring == 0:
            dkv_ref[0, other] = dkv
        else:
            dkv_ref[0, other, :, :prefix] += dkv


def back_far(qa, do, kv, far, bias):
    heads, blocks = kv.shape[:2]
    local_rings = blocks.bit_length() - 1
    rows = SEGMENT_TILES >> (local_rings + 1)
    whole = lambda shape: pl.BlockSpec((1,) + shape[1:], lambda h: (h,) + (0,) * (len(shape) - 1))
    pairs = heads * blocks * rows * 2600
    turned = (heads, blocks, LANES, SEGMENT_TILES)
    return pl.pallas_call(
        functools.partial(back_far_kernel, local_rings, blocks),
        grid=(heads,),
        in_specs=[
            whole(qa.shape),
            pl.BlockSpec((1, blocks, rows, LANES), lambda h: (h, 0, 0, 0)),
            whole(kv.shape),
            whole(far.shape),
            whole(bias.shape),
        ],
        out_specs=[whole(qa.shape), whole(turned), whole(far.shape)],
        out_shape=[
            jax.ShapeDtypeStruct(qa.shape, F32),
            jax.ShapeDtypeStruct(turned, F32),
            jax.ShapeDtypeStruct(far.shape, BF16),
        ],
        cost_estimate=pl.CostEstimate(
            flops=pairs * 2560, bytes_accessed=heads * 6 * 1024 * 1024, transcendentals=pairs
        ),
        compiler_params=pltpu.CompilerParams(vmem_limit_bytes=VMEM_LIMIT),
        name="back_far",
    )(qa, do, kv, far, bias)


def collect_kernel(heads, row_count, counts, score_scale, base_ref, *refs):
    dq_far_ref, dq_near_ref, one_ref, two_ref = refs[:4]
    returned = refs[4 : 4 + len(counts)]
    out_ref, held_ref = refs[4 + len(counts) :]
    piece = row_count // RESIDUES
    halves = SEGMENT_TILES // row_count
    far_rows = dq_far_ref.shape[2]
    for head in range(heads):
        held_ref[...] = (one_ref[head, 0] + two_ref[head, 0]).T
        for back_ref, count in zip(returned, counts):
            held_ref[:count, :] += back_ref[head, 0].astype(F32)
        lane = lax.broadcasted_iota(jnp.int32, (piece, LANES), 1)
        factor = jnp.where(lane < HEAD_WIDTH, LN2, jnp.where(lane < SUM_LANE, 1.0, 0.0))
        q_factor = jnp.where(lane < HEAD_WIDTH, score_scale, 0.0)
        for slab in range(RESIDUES):
            residue = lax.rem(base_ref[0] + head + ORDER[slab], RESIDUES)
            for half in range(halves):
                start = slab * SLAB + half * piece
                if start < far_rows:
                    value = dq_far_ref[head, 0, start : start + piece, :]
                else:
                    value = dq_near_ref[head, 0, start - far_rows : start - far_rows + piece, :]
                target = pl.ds(pl.multiple_of(half * row_count + residue * piece, piece), piece)
                at = head * 2 * LANES
                out_ref[target, at : at + LANES] = (value * q_factor).astype(BF16)
                out_ref[target, at + LANES : at + 2 * LANES] = (
                    held_ref[start : start + piece, :] * factor
                ).astype(BF16)


def collect(base, dq_far, dq_near, dkv_one, dkv_two, returned, row_count, score_scale):
    heads, blocks = dq_far.shape[:2]
    counts = tuple(one.shape[2] for one in returned)
    part = lambda shape: pl.BlockSpec((heads, 1) + shape[2:], lambda k, *_: (0, k, 0, 0))
    arrays = (dq_far, dq_near, dkv_one, dkv_two) + tuple(returned)
    width = heads * 2 * LANES
    return pl.pallas_call(
        functools.partial(collect_kernel, heads, row_count, counts, score_scale),
        grid_spec=pltpu.PrefetchScalarGridSpec(
            num_scalar_prefetch=1,
            grid=(blocks,),
            in_specs=[part(one.shape) for one in arrays],
            out_specs=pl.BlockSpec((SEGMENT_TILES, width), lambda k, *_: (k, 0)),
            scratch_shapes=[pltpu.VMEM((SEGMENT_TILES, LANES), F32)],
        ),
        out_shape=jax.ShapeDtypeStruct((blocks * SEGMENT_TILES, width), BF16),
        cost_estimate=pl.CostEstimate(
            flops=blocks * SEGMENT_TILES * width * 8,
            bytes_accessed=blocks * SEGMENT_TILES * width * 10,
            transcendentals=0,
        ),
        compiler_params=pltpu.CompilerParams(vmem_limit_bytes=VMEM_LIMIT),
        name="collect",
    )(base, *arrays)


def residue_major(rows):
    count, width = rows.shape
    return rows.reshape(count // RESIDUES, RESIDUES, width).swapaxes(0, 1).reshape(count, width)


def position_major(rows):
    count, width = rows.shape
    return rows.reshape(RESIDUES, count // RESIDUES, width).swapaxes(0, 1).reshape(count, width)


def norm_forward(values, norm_gain, norm_shift):
    center = values - jnp.mean(values, axis=-1, keepdims=True)
    inverse = lax.rsqrt(jnp.mean(center * center, axis=-1, keepdims=True) + epsilon)
    normed = center * inverse
    return (normed * norm_gain + norm_shift, normed, inverse)


def norm_backward(grad_out, normed, inverse, norm_gain):
    scaled = grad_out * norm_gain
    return inverse * (
        scaled
        - jnp.mean(scaled, axis=-1, keepdims=True)
        - normed * jnp.mean(scaled * normed, axis=-1, keepdims=True)
    )


def gelu_tanh(values):
    return jax.nn.gelu(values, approximate=True)


def from_other(x, axis, flip):
    return lax.ppermute(x, axis, [(i, i ^ flip) for i in range(lax.axis_size(axis))])


def exchange(parts, axis):
    count = lax.axis_size(axis)
    rank = lax.axis_index(axis)
    found = [lax.dynamic_index_in_dim(parts, rank, 0, keepdims=False)]
    for flip in range(1, count):
        sent = lax.dynamic_index_in_dim(parts, rank ^ flip, 0, keepdims=False)
        found.append(from_other(sent, axis, flip))
    return jnp.stack(found)[rank ^ jnp.arange(count)]


def per_device(
    tile_features,
    slide_lengths,
    qkv_weight,
    qv_bias,
    out_weight,
    out_bias,
    attn_gain,
    attn_shift,
    mlp_gain,
    mlp_shift,
    up_weight,
    up_bias,
    down_weight,
    down_bias,
    output_cotangent,
):
    row_count = tile_features.shape[2]
    width = tile_features.shape[3]
    local_width = qkv_weight.shape[2]
    heads = local_width // HEAD_WIDTH
    sequence_member = lax.axis_index("seq")
    head_rank = lax.axis_index("head")
    head_count = lax.axis_size("head")
    extent = row_count * head_count
    blocks = extent // SEGMENT_TILES
    local_rings = blocks.bit_length() - 1
    score_scale = HEAD_WIDTH ** (-0.5)
    query_scale = score_scale / LN2
    base = (head_rank * heads).astype(jnp.int32).reshape(1)

    features = residue_major(tile_features.reshape(row_count, width)).astype(F32)
    normed_one, hat_one, inv_one = norm_forward(features, attn_gain, attn_shift)
    normed_one = normed_one.astype(BF16)
    gathered_one = lax.all_gather(normed_one, "head", axis=0, tiled=True)

    by_head = qkv_weight.reshape(width, 3, heads, HEAD_WIDTH)
    query_weight = jnp.pad(by_head[:, 0], ((0, 0), (0, 0), (0, LANES - HEAD_WIDTH)))
    pair_weight = jnp.pad(
        jnp.concatenate([by_head[:, 1], by_head[:, 2]], axis=-1),
        ((0, 0), (0, 0), (0, LANES - 2 * HEAD_WIDTH)),
    )
    wide = jnp.concatenate([query_weight, pair_weight], axis=-1).reshape(width, heads * 2 * LANES)
    scale_row = np.ones((heads, 2 * LANES), np.float32)
    scale_row[:, :HEAD_WIDTH] = query_scale
    by_head_bias = qv_bias.reshape(2, heads, HEAD_WIDTH)
    ones = np.zeros((heads, LANES - 2 * HEAD_WIDTH), np.float32)
    ones[:, : 1 + AUX_COUNT] = 1.0
    wide_bias = jnp.concatenate(
        [
            by_head_bias[0],
            jnp.zeros((heads, LANES - HEAD_WIDTH), F32),
            jnp.zeros((heads, HEAD_WIDTH), F32),
            by_head_bias[1],
            jnp.asarray(ones),
        ],
        axis=1,
    ).reshape(1, heads * 2 * LANES)
    scale_row = jnp.asarray(scale_row).reshape(1, heads * 2 * LANES)
    bias = key_bias(slide_lengths, sequence_member, head_rank * heads, heads, blocks, row_count)

    q, kv = project(
        base, gathered_one, wide, jnp.concatenate([wide_bias, scale_row], axis=0), heads, row_count
    )
    received = []
    for ring in range(local_rings + 1, LEVELS):
        prefix = SEGMENT_TILES >> ring
        sent = kv[:, :, :prefix].reshape(heads, blocks * prefix, LANES)
        for flip in ring_members(ring, blocks):
            received.append(from_other(sent, "seq", flip))
    up_all = lax.all_gather(up_weight, "head", axis=0)
    down_all = lax.all_gather(down_weight, "head", axis=0)
    out_all = lax.all_gather(out_weight, "head", axis=0, tiled=True)
    up_bias_all = lax.all_gather(up_bias, "head", axis=0)

    o_near, qa_near = attend_near(q, kv, bias)
    far = jnp.concatenate(received, axis=1)
    o_far, qa_far = attend_far(q, kv, far, bias)
    packed = pack(base, o_far, o_near, row_count)
    attn_parts = exchange(packed.reshape(head_count, row_count, local_width), "head")
    attn_low = attn_parts.swapaxes(0, 1).reshape(row_count, width)

    residual = features + dot(attn_low, out_all, 1, 0) + out_bias
    normed_two, hat_two, inv_two = norm_forward(residual, mlp_gain, mlp_shift)
    normed_two = normed_two.astype(BF16)
    cotangent = residue_major(output_cotangent.reshape(row_count, width))
    result = residual + down_bias
    grad_normed_two = 0.0
    grad_up, grad_down, grad_up_bias = [], [], []
    for part in range(head_count):
        pre_act = dot(normed_two, up_all[part], 1, 0) + up_bias_all[part]
        hidden = gelu_tanh(pre_act).astype(BF16)
        result = result + dot(hidden, down_all[part], 1, 0)
        grad_hidden = dot(cotangent, down_all[part], 1, 1)
        grad_down.append(dot(hidden, cotangent, 0, 0).astype(BF16))
        grad_pre = jax.vjp(gelu_tanh, pre_act)[1](grad_hidden)[0].astype(BF16)
        grad_up_bias.append(jnp.sum(grad_pre.astype(F32), axis=0))
        grad_up.append(dot(normed_two, grad_pre, 0, 0).astype(BF16))
        grad_normed_two = grad_normed_two + dot(grad_pre, up_all[part], 1, 1)
    output = position_major(result.astype(BF16)).reshape(tile_features.shape)
    grad_result = cotangent.astype(F32)
    grad_mlp_gain = jnp.sum(grad_normed_two * hat_two, axis=0)
    grad_mlp_shift = jnp.sum(grad_normed_two, axis=0)
    grad_residual = grad_result + norm_backward(grad_normed_two, hat_two, inv_two, mlp_gain)
    grad_down_bias = jnp.sum(grad_result, axis=0)
    grad_out_bias = jnp.sum(grad_residual, axis=0)
    grad_res_low = grad_residual.astype(BF16)
    grad_attn = dot(grad_res_low, out_all, 1, 1).astype(BF16)
    grad_parts = exchange(
        grad_attn.reshape(row_count, head_count, local_width).swapaxes(0, 1), "head"
    ).reshape(extent, local_width)
    grad_out = dot(attn_low, grad_res_low, 0, 0).astype(BF16)

    do = unpack(base, grad_parts, o_far, o_near, row_count)
    dq_far, dkv_far, dfar = back_far(qa_far, do, kv, far, bias)
    returned = []
    at = 0
    for ring in range(local_rings + 1, LEVELS):
        prefix = SEGMENT_TILES >> ring
        for flip in ring_members(ring, blocks):
            sent = dfar[:, at : at + blocks * prefix]
            at += blocks * prefix
            returned.append(
                from_other(sent, "seq", flip).reshape(heads, blocks, prefix, LANES)
            )
    dq_near, dkv_near = back_near(qa_near, do, kv, bias)

    scatter = lambda x: lax.psum_scatter(x, "head", scatter_dimension=0, tiled=False)
    grad_up = lax.psum(scatter(jnp.stack(grad_up)), "seq").astype(F32)
    grad_down = lax.psum(scatter(jnp.stack(grad_down)), "seq").astype(F32)
    grad_out = lax.psum(
        scatter(grad_out.reshape(head_count, local_width, width)), "seq"
    ).astype(F32)
    grad_up_bias = lax.psum(scatter(jnp.stack(grad_up_bias)), "seq")

    grad_proj = collect(base, dq_far, dq_near, dkv_far, dkv_near, returned, row_count, score_scale)
    part_sums = jnp.sum(grad_proj.astype(F32), axis=0).reshape(heads, 2, LANES)
    grad_qv = jnp.stack(
        [
            part_sums[:, 0, :HEAD_WIDTH].reshape(local_width),
            part_sums[:, 1, HEAD_WIDTH : 2 * HEAD_WIDTH].reshape(local_width),
        ]
    )
    grad_wide = dot(gathered_one, grad_proj, 0, 0).reshape(width, heads, 2, LANES)
    grad_qkv = jnp.stack(
        [
            grad_wide[:, :, 0, :HEAD_WIDTH].reshape(width, local_width),
            grad_wide[:, :, 1, :HEAD_WIDTH].reshape(width, local_width),
            grad_wide[:, :, 1, HEAD_WIDTH : 2 * HEAD_WIDTH].reshape(width, local_width),
        ],
        axis=1,
    )
    grad_normed_one = lax.psum_scatter(
        dot(grad_proj, wide, 1, 1).astype(BF16), "head", scatter_dimension=0, tiled=True
    ).astype(F32)
    grad_attn_gain = jnp.sum(grad_normed_one * hat_one, axis=0)
    grad_attn_shift = jnp.sum(grad_normed_one, axis=0)
    grad_features = grad_residual + norm_backward(grad_normed_one, hat_one, inv_one, attn_gain)
    grad_qkv = lax.psum(grad_qkv.astype(BF16), "seq").astype(F32)
    grad_qv = lax.psum(grad_qv, "seq")
    norm_totals = lax.psum(
        (
            grad_attn_gain,
            grad_attn_shift,
            grad_mlp_gain,
            grad_mlp_shift,
            grad_out_bias,
            grad_down_bias,
        ),
        ("head", "seq"),
    )
    return (
        output,
        position_major(grad_features).reshape(tile_features.shape),
        grad_qkv,
        grad_qv,
        grad_out,
        norm_totals[4],
        norm_totals[0],
        norm_totals[1],
        norm_totals[2],
        norm_totals[3],
        grad_up,
        grad_up_bias,
        grad_down,
        norm_totals[5],
    )


def solution(mesh):
    in_specs = (
        P("seq", "head", None, None),
        P(),
        P(None, None, "head"),
        P(None, "head"),
        P("head", None),
        P(),
        P(),
        P(),
        P(),
        P(),
        P(None, "head"),
        P("head"),
        P("head", None),
        P(),
        P("seq", "head", None, None),
    )
    out_specs = (
        P("seq", "head", None, None),
        P("seq", "head", None, None),
        P(None, None, "head"),
        P(None, "head"),
        P("head", None),
        P(),
        P(),
        P(),
        P(),
        P(),
        P(None, "head"),
        P("head"),
        P("head", None),
        P(),
    )
    return jax.shard_map(
        per_device, mesh=mesh, in_specs=in_specs, out_specs=out_specs, check_vma=False
    )
```

```python
import functools
import math

import jax
import jax.numpy as jnp
import numpy as np
from jax import lax
from jax.experimental import pallas as pl
from jax.experimental.pallas import tpu as pltpu
from jax.sharding import PartitionSpec as P

HEAD_WIDTH = 48
SEGMENT_TILES = 1024
LEVELS = 5
RESIDUES = 16
LANES = 128
RING_KEYS = SEGMENT_TILES // 2
ORDER = (0, 8, 4, 12, 2, 6, 10, 14, 1, 3, 5, 7, 9, 11, 13, 15)
SLAB = SEGMENT_TILES // RESIDUES

epsilon = 1e-05
masked_low = -1e30
BF16 = jnp.bfloat16
F32 = jnp.float32
MESH = pl.DeviceIdType.MESH
LN2 = math.log(2.0)
SEQ = ("pair", "core")
EVERY = ("head", "pair", "core")
SUM_LANE = 2 * HEAD_WIDTH
AUX_LANE = SUM_LANE + 1
AUX_COUNT = 3
VMEM_LIMIT = 52 * 1024 * 1024


def dot(left_side, right_side, left_dim, right_dim):
    return lax.dot_general(
        left_side,
        right_side,
        (((left_dim,), (right_dim,)), ((), ())),
        preferred_element_type=F32,
    )


def class_rows(level):
    low = SEGMENT_TILES >> (level + 1) if level < LEVELS - 1 else 0
    return low, SEGMENT_TILES >> level


def key_class():
    index = np.arange(SEGMENT_TILES)
    found = np.zeros(SEGMENT_TILES, np.int64)
    for level in range(LEVELS):
        found[index < SEGMENT_TILES >> level] = level
    return found


def multiplicity_table():
    classes = key_class()
    table = np.zeros((LEVELS, SEGMENT_TILES + (LEVELS - 1) * RING_KEYS), np.float32)
    for level in range(LEVELS):
        table[level, :SEGMENT_TILES] = 1 + np.minimum(level, classes)
        for ring in range(1, level + 1):
            prefix = SEGMENT_TILES >> ring
            one = np.minimum(level, classes[:prefix]) - ring + 1
            start = SEGMENT_TILES + (ring - 1) * RING_KEYS
            table[level, start : start + RING_KEYS] = np.tile(one, RING_KEYS // prefix)
    return table


def layout(slide_lengths, positions):
    blocks = (slide_lengths + SEGMENT_TILES - 1) // SEGMENT_TILES
    slide_ends = jnp.cumsum(blocks) * SEGMENT_TILES
    slide_starts = slide_ends - blocks * SEGMENT_TILES
    inside = (positions[..., None] >= slide_starts) & (positions[..., None] < slide_ends)
    labels = jnp.arange(slide_lengths.shape[0], dtype=jnp.int32)
    slide_index = jnp.sum(jnp.where(inside, labels, 0), axis=-1)
    offset = positions - jnp.sum(jnp.where(inside, slide_starts, 0), axis=-1)
    length = jnp.sum(jnp.where(inside, slide_lengths, 0), axis=-1)
    return (slide_index, offset < length)


def ring_members(ring, block_count):
    return range((1 << (ring - 1)) // block_count, (1 << ring) // block_count)


def key_bias(slide_lengths, sequence_member, base_head, heads, block_count, row_count):
    local_rings = block_count.bit_length() - 1
    index = np.arange(SEGMENT_TILES)
    order = np.asarray(ORDER)[index // SLAB]
    piece = row_count // RESIDUES
    spot = (index % SLAB) // piece * row_count + index % piece * RESIDUES
    head = base_head + jnp.arange(heads, dtype=jnp.int32)[:, None]
    inner = spot[None, :] + (head + order[None, :]) % RESIDUES
    first_block = sequence_member * block_count
    per_block = []
    for block in range(block_count):
        parts = [(first_block + block) * SEGMENT_TILES + inner]
        for ring in range(1, LEVELS):
            prefix = SEGMENT_TILES >> ring
            if ring <= local_rings:
                start = (block >> (ring - 1) ^ 1) << (ring - 1)
                ids = [first_block + start + t for t in range(1 << (ring - 1))]
            else:
                ids = [
                    (sequence_member ^ x) * block_count + t
                    for x in ring_members(ring, block_count)
                    for t in range(block_count)
                ]
            parts += [one * SEGMENT_TILES + inner[:, :prefix] for one in ids]
        per_block.append(jnp.concatenate(parts, axis=1))
    positions = jnp.stack(per_block, axis=1).astype(jnp.int32)
    slide, valid = layout(slide_lengths, positions)
    own, _ = layout(
        slide_lengths,
        (first_block + jnp.arange(block_count, dtype=jnp.int32)) * SEGMENT_TILES,
    )
    allowed = (slide == own[None, :, None]) & valid
    table = multiplicity_table()
    logs = np.where(table > 0, np.log2(np.maximum(table, 1)), masked_low).astype(np.float32)
    return jnp.where(allowed[:, :, None, :], logs[None, None], masked_low)


def project_kernel(heads, row_count, base_ref, x_ref, w_ref, b_ref, q_ref, kv_ref, held_ref):
    piece = row_count // RESIDUES
    halves = SEGMENT_TILES // row_count
    for half in range(halves):
        x = x_ref[half * row_count : (half + 1) * row_count, :]
        for head in range(heads):
            columns = slice(head * 2 * LANES, (head + 1) * 2 * LANES)
            wide = dot(x, w_ref[:, columns], 1, 0) + b_ref[0:1, columns]
            held_ref[...] = (wide * b_ref[1:2, columns]).astype(BF16)
            for slab in range(RESIDUES):
                residue = lax.rem(base_ref[0] + head + ORDER[slab], RESIDUES)
                source = pl.ds(pl.multiple_of(residue * piece, piece), piece)
                start = slab * SLAB + half * piece
                q_ref[head, 0, start : start + piece, :] = held_ref[source, :LANES]
                kv_ref[head, 0, start : start + piece, :] = held_ref[source, LANES:]


def project(base, rows, weight, bias, heads, row_count):
    total, width = rows.shape
    blocks = total // SEGMENT_TILES
    shape = jax.ShapeDtypeStruct((heads, blocks, SEGMENT_TILES, LANES), BF16)
    spec = pl.BlockSpec((heads, 1, SEGMENT_TILES, LANES), lambda k, *_: (0, k, 0, 0))
    return pl.pallas_call(
        functools.partial(project_kernel, heads, row_count),
        grid_spec=pltpu.PrefetchScalarGridSpec(
            num_scalar_prefetch=1,
            grid=(blocks,),
            in_specs=[
                pl.BlockSpec((SEGMENT_TILES, width), lambda k, *_: (k, 0)),
                pl.BlockSpec(weight.shape, lambda k, *_: (0, 0)),
                pl.BlockSpec(bias.shape, lambda k, *_: (0, 0)),
            ],
            out_specs=[spec, spec],
            scratch_shapes=[pltpu.VMEM((row_count, 2 * LANES), BF16)],
        ),
        out_shape=[shape, shape],
        cost_estimate=pl.CostEstimate(
            flops=2 * total * width * weight.shape[1], bytes_accessed=8 * total * width, transcendentals=0
        ),
        compiler_params=pltpu.CompilerParams(vmem_limit_bytes=VMEM_LIMIT),
        name="project",
    )(base, rows, weight, bias)


def split_three(value):
    high = value.astype(BF16).astype(F32)
    rest = value - high
    middle = rest.astype(BF16).astype(F32)
    return high, middle, rest - middle


def split_exact(value):
    high = lax.reduce_precision(value, 8, 7)
    middle = lax.reduce_precision(value - high, 8, 7)
    return high, middle, lax.reduce_precision(value - high - middle, 8, 7)


def with_aux(rows, value):
    lane = lax.broadcasted_iota(jnp.int32, rows.shape, 1)
    filled = rows.astype(F32)
    for step, part in enumerate(split_three(value)):
        filled = jnp.where(lane == AUX_LANE + step, part, filled)
    return filled.astype(BF16)


def finish(total, peak, q):
    denominator = total[:, SUM_LANE : SUM_LANE + 1]
    lse = peak + jnp.log(denominator) * (1.0 / LN2)
    return total / denominator, with_aux(q, -lse)


def local_pieces(kv_ref, block, ring):
    count = 1 << (ring - 1)
    start = (block // count) ^ 1
    prefix = SEGMENT_TILES >> ring
    return [(start * count + t, prefix) for t in range(count)]


def attend_near_kernel(local_rings, q_ref, kv_ref, bias_ref, o_ref, qa_ref):
    block = pl.program_id(1)
    first = SEGMENT_TILES >> (local_rings + 1)
    for level in range(local_rings + 1):
        low, high = class_rows(level)
        size = min(256, high - low)
        for start in range(low, high, size):
            q = q_ref[0, 0, start : start + size, :]
            keys = [(kv_ref[0, block], 0)]
            place = SEGMENT_TILES
            for ring in range(1, level + 1):
                for other, prefix in local_pieces(kv_ref, block, ring):
                    keys.append((kv_ref[0, other, :prefix], place))
                    place += prefix
            scores = [
                dot(q, kv, 1, 1) + bias_ref[0, 0, level : level + 1, at : at + kv.shape[0]]
                for kv, at in keys
            ]
            peak = functools.reduce(
                jnp.maximum, [jnp.max(s, axis=1, keepdims=True) for s in scores]
            )
            total = sum(
                dot(jnp.exp2(s - peak).astype(BF16), kv, 1, 0) for s, (kv, _) in zip(scores, keys)
            )
            out, extended = finish(total, peak, q)
            o_ref[0, 0, start - first : start - first + size, :] = out
            qa_ref[0, 0, start - first : start - first + size, :] = extended


def attend_near(q, kv, bias):
    heads, blocks = q.shape[:2]
    local_rings = blocks.bit_length() - 1
    rows = SEGMENT_TILES - (SEGMENT_TILES >> (local_rings + 1))
    spec = pl.BlockSpec((1, 1, rows, LANES), lambda h, k: (h, k, 0, 0))
    pairs = heads * blocks * rows * 1400
    return pl.pallas_call(
        functools.partial(attend_near_kernel, local_rings),
        grid=(heads, blocks),
        in_specs=[
            pl.BlockSpec((1, 1, SEGMENT_TILES, LANES), lambda h, k: (h, k, 0, 0)),
            pl.BlockSpec((1, blocks, SEGMENT_TILES, LANES), lambda h, k: (h, 0, 0, 0)),
            pl.BlockSpec((1, 1) + bias.shape[2:], lambda h, k: (h, k, 0, 0)),
        ],
        out_specs=[spec, spec],
        out_shape=[
            jax.ShapeDtypeStruct((heads, blocks, rows, LANES), F32),
            jax.ShapeDtypeStruct((heads, blocks, rows, LANES), BF16),
        ],
        cost_estimate=pl.CostEstimate(
            flops=pairs * 1024, bytes_accessed=heads * blocks * rows * 1500, transcendentals=pairs
        ),
        compiler_params=pltpu.CompilerParams(vmem_limit_bytes=VMEM_LIMIT),
        name="attend_near",
    )(q, kv, bias)


def far_groups(local_rings):
    groups = []
    for level in range(local_rings + 1, LEVELS):
        low, high = class_rows(level)
        groups.append((level, low, high))
    return sorted(groups, key=lambda group: group[1])


def add_bias(scores, bias_ref, block, at, groups, rows):
    width = scores.shape[1]
    parts = []
    for level, low, high in groups:
        if low < rows:
            parts.append(scores[low:high] + bias_ref[0, block, level : level + 1, at : at + width])
    return parts[0] if len(parts) == 1 else jnp.concatenate(parts, axis=0)


def far_score_list(local_rings, blocks, left_ref, kv_ref, far_ref):
    rows = SEGMENT_TILES >> (local_rings + 1)
    pieces = []
    for block in range(blocks):
        pieces.append((0, block, block, SEGMENT_TILES, rows, 0))
    for block in range(blocks):
        place = SEGMENT_TILES
        for ring in range(1, local_rings + 1):
            for other, prefix in local_pieces(kv_ref, block, ring):
                pieces.append((ring, block, other, prefix, rows, place))
                place += prefix
    for ring in range(local_rings + 1, LEVELS):
        pieces.append((ring, None, None, RING_KEYS, SEGMENT_TILES >> ring, SEGMENT_TILES + (ring - 1) * RING_KEYS))
    return pieces


def far_keys(piece, kv_ref, far_ref, local_rings):
    ring, block, other, prefix, rows, place = piece
    if block is not None:
        return kv_ref[0, other, :prefix]
    start = (ring - local_rings - 1) * RING_KEYS
    return far_ref[0, start : start + RING_KEYS, :]


def far_left(piece, left_ref, blocks):
    ring, block, other, prefix, rows, place = piece
    if block is not None:
        return left_ref[0, block, :rows, :]
    return jnp.concatenate([left_ref[0, one, :rows, :] for one in range(blocks)], axis=0)


def pad_rows(value, rows, fill):
    if value.shape[0] == rows:
        return value
    return jnp.concatenate(
        [value, jnp.full((rows - value.shape[0],) + value.shape[1:], fill, value.dtype)], axis=0
    )


def attend_far_kernel(local_rings, blocks, q_ref, kv_ref, far_ref, bias_ref, o_ref, qa_ref):
    rows = SEGMENT_TILES >> (local_rings + 1)
    groups = far_groups(local_rings)
    pieces = far_score_list(local_rings, blocks, q_ref, kv_ref, far_ref)
    held = []
    peaks = [None] * blocks
    for piece in pieces:
        ring, block, other, prefix, count, place = piece
        scores = dot(far_left(piece, q_ref, blocks), far_keys(piece, kv_ref, far_ref, local_rings), 1, 1)
        for one in [block] if block is not None else range(blocks):
            part = scores if block is not None else scores[one * count : (one + 1) * count]
            part = add_bias(part, bias_ref, one, place, groups, count)
            held.append((piece, one, part))
            top = pad_rows(jnp.max(part, axis=1, keepdims=True), rows, masked_low)
            peaks[one] = top if peaks[one] is None else jnp.maximum(peaks[one], top)
    totals = [jnp.zeros((rows, LANES), F32)] * blocks
    for piece in pieces:
        weights = [
            (one, jnp.exp2(part - peaks[one][: piece[4]]).astype(BF16))
            for owner, one, part in held
            if owner is piece
        ]
        joined = weights[0][1] if len(weights) == 1 else jnp.concatenate([w for _, w in weights], axis=0)
        product = dot(joined, far_keys(piece, kv_ref, far_ref, local_rings), 1, 0)
        for at, (one, _) in enumerate(weights):
            part = product[at * piece[4] : (at + 1) * piece[4]]
            totals[one] = totals[one] + pad_rows(part, rows, 0.0)
    for block in range(blocks):
        out, extended = finish(totals[block], peaks[block], q_ref[0, block, :rows, :])
        o_ref[0, block] = out
        qa_ref[0, block] = extended


def attend_far(q, kv, far, bias):
    heads, blocks = q.shape[:2]
    local_rings = blocks.bit_length() - 1
    rows = SEGMENT_TILES >> (local_rings + 1)
    whole = lambda shape: pl.BlockSpec((1,) + shape[1:], lambda h: (h,) + (0,) * (len(shape) - 1))
    shape = (heads, blocks, rows, LANES)
    pairs = heads * blocks * rows * 2600
    return pl.pallas_call(
        functools.partial(attend_far_kernel, local_rings, blocks),
        grid=(heads,),
        in_specs=[
            pl.BlockSpec((1, blocks, rows, LANES), lambda h: (h, 0, 0, 0)),
            whole(kv.shape),
            whole(far.shape),
            whole(bias.shape),
        ],
        out_specs=[whole(shape), whole(shape)],
        out_shape=[jax.ShapeDtypeStruct(shape, F32), jax.ShapeDtypeStruct(shape, BF16)],
        cost_estimate=pl.CostEstimate(
            flops=pairs * 1024, bytes_accessed=heads * 4 * 1024 * 1024, transcendentals=pairs
        ),
        compiler_params=pltpu.CompilerParams(vmem_limit_bytes=VMEM_LIMIT),
        name="attend_far",
    )(q, kv, far, bias)


def placement(heads):
    table = np.zeros((heads * LANES, heads * HEAD_WIDTH), np.float32)
    for head in range(heads):
        for column in range(HEAD_WIDTH):
            table[head * LANES + HEAD_WIDTH + column, head * HEAD_WIDTH + column] = 1
    return table


def pair_placement(width):
    table = np.zeros((2, width, 2 * width), np.float32)
    column = np.arange(width)
    table[0, column, column] = 1
    table[1, column, width + column] = 1
    return table


def side_by_side(rows, table_ref):
    half = rows.shape[0] // 2
    return dot(rows[:half], table_ref[0], 1, 0) + dot(rows[half:], table_ref[1], 1, 0)


def pack_kernel(heads, row_count, base_ref, far_ref, near_ref, place_ref, out_ref, held_ref):
    piece = row_count // RESIDUES
    halves = SEGMENT_TILES // row_count
    far_rows = far_ref.shape[2]
    for head in range(heads):
        columns = slice(head * LANES, (head + 1) * LANES)
        for slab in range(RESIDUES):
            residue = lax.rem(base_ref[0] + head + ORDER[slab], RESIDUES)
            for half in range(halves):
                start = slab * SLAB + half * piece
                if start < far_rows:
                    value = far_ref[head, 0, start : start + piece, :]
                else:
                    value = near_ref[head, 0, start - far_rows : start - far_rows + piece, :]
                target = pl.ds(pl.multiple_of(half * row_count + residue * piece, piece), piece)
                held_ref[target, columns] = value.astype(BF16)
    for half in range(halves):
        rows = held_ref[half * row_count : (half + 1) * row_count, :]
        out_ref[half] = side_by_side(rows, place_ref).astype(BF16)


def pack_table(heads):
    pairs = pair_placement(heads * HEAD_WIDTH)
    return jnp.asarray(np.stack([placement(heads) @ one for one in pairs]), BF16)


def pack(base, far, near, row_count):
    heads, blocks = far.shape[:2]
    place = pack_table(heads)
    width = heads * HEAD_WIDTH
    halves = SEGMENT_TILES // row_count
    part = lambda shape: pl.BlockSpec((heads, 1) + shape[2:], lambda k, *_: (0, k, 0, 0))
    return pl.pallas_call(
        functools.partial(pack_kernel, heads, row_count),
        grid_spec=pltpu.PrefetchScalarGridSpec(
            num_scalar_prefetch=1,
            grid=(blocks,),
            in_specs=[part(far.shape), part(near.shape), pl.BlockSpec(place.shape, lambda k, *_: (0, 0, 0))],
            out_specs=pl.BlockSpec((halves, row_count // 2, 2 * width), lambda k, *_: (k, 0, 0)),
            scratch_shapes=[pltpu.VMEM((SEGMENT_TILES, heads * LANES), BF16)],
        ),
        out_shape=jax.ShapeDtypeStruct((blocks * halves, row_count // 2, 2 * width), BF16),
        cost_estimate=pl.CostEstimate(
            flops=2 * blocks * SEGMENT_TILES * heads * LANES * width,
            bytes_accessed=blocks * SEGMENT_TILES * heads * LANES * 5,
            transcendentals=0,
        ),
        compiler_params=pltpu.CompilerParams(vmem_limit_bytes=VMEM_LIMIT),
        name="pack",
    )(base, far, near, place)


def unpack_kernel(heads, row_count, base_ref, g_ref, far_ref, near_ref, place_ref, out_ref, held_ref):
    piece = row_count // RESIDUES
    halves = SEGMENT_TILES // row_count
    far_rows = far_ref.shape[2]
    for half in range(halves):
        for side in range(2):
            start = half * row_count + side * (row_count // 2)
            held_ref[start : start + row_count // 2, :] = dot(g_ref[half], place_ref[side], 1, 1)
    for head in range(heads):
        columns = slice(head * LANES, (head + 1) * LANES)
        for slab in range(RESIDUES):
            residue = lax.rem(base_ref[0] + head + ORDER[slab], RESIDUES)
            for half in range(halves):
                start = slab * SLAB + half * piece
                if start < far_rows:
                    value = far_ref[head, 0, start : start + piece, :]
                else:
                    value = near_ref[head, 0, start - far_rows : start - far_rows + piece, :]
                source = pl.ds(pl.multiple_of(half * row_count + residue * piece, piece), piece)
                grad = held_ref[source, columns]
                delta = jnp.sum(grad * value, axis=1, keepdims=True)
                out_ref[head, 0, start : start + piece, :] = with_aux(grad, -delta)


def unpack(base, grad, far, near, row_count):
    heads, blocks = far.shape[:2]
    place = pack_table(heads)
    width = heads * HEAD_WIDTH
    halves = SEGMENT_TILES // row_count
    part = lambda shape: pl.BlockSpec((heads, 1) + shape[2:], lambda k, *_: (0, k, 0, 0))
    shape = (heads, blocks, SEGMENT_TILES, LANES)
    return pl.pallas_call(
        functools.partial(unpack_kernel, heads, row_count),
        grid_spec=pltpu.PrefetchScalarGridSpec(
            num_scalar_prefetch=1,
            grid=(blocks,),
            in_specs=[
                pl.BlockSpec((halves, row_count // 2, 2 * width), lambda k, *_: (k, 0, 0)),
                part(far.shape),
                part(near.shape),
                pl.BlockSpec(place.shape, lambda k, *_: (0, 0, 0)),
            ],
            out_specs=part(shape),
            scratch_shapes=[pltpu.VMEM((SEGMENT_TILES, heads * LANES), F32)],
        ),
        out_shape=jax.ShapeDtypeStruct(shape, BF16),
        cost_estimate=pl.CostEstimate(
            flops=2 * blocks * SEGMENT_TILES * heads * LANES * width,
            bytes_accessed=blocks * SEGMENT_TILES * heads * LANES * 7,
            transcendentals=0,
        ),
        compiler_params=pltpu.CompilerParams(vmem_limit_bytes=VMEM_LIMIT),
        name="unpack",
    )(base, grad, far, near, place)


def back_near_kernel(local_rings, qa_ref, do_ref, kv_ref, bias_ref, dq_ref, dkv_ref):
    block = pl.program_id(1)
    first = SEGMENT_TILES >> (local_rings + 1)

    @pl.when(block == 0)
    def _():
        dkv_ref[...] = jnp.zeros_like(dkv_ref)

    for level in range(local_rings + 1):
        low, high = class_rows(level)
        size = min(256, high - low)
        for start in range(low, high, size):
            here = slice(start - first, start - first + size)
            q = qa_ref[0, 0, here, :]
            grad = do_ref[0, 0, start : start + size, :]
            q_turned, grad_turned = q.T, grad.T
            keys = [(block, SEGMENT_TILES, 0)]
            place = SEGMENT_TILES
            for ring in range(1, level + 1):
                for other, prefix in local_pieces(kv_ref, block, ring):
                    keys.append((other, prefix, place))
                    place += prefix
            dq = jnp.zeros((size, LANES), F32)
            for other, prefix, at in keys:
                kv = kv_ref[0, other, :prefix]
                scores = dot(q, kv, 1, 1) + bias_ref[0, 0, level : level + 1, at : at + prefix]
                weights = jnp.exp2(scores)
                grads = (weights * dot(grad, kv, 1, 1)).astype(BF16)
                dq = dq + dot(grads, kv, 1, 0)
                dkv_ref[0, other, :, :prefix] += dot(q_turned, grads, 1, 0) + dot(
                    grad_turned, weights.astype(BF16), 1, 0
                )
            dq_ref[0, 0, here, :] = dq


def back_near(qa, do, kv, bias):
    heads, blocks = kv.shape[:2]
    local_rings = blocks.bit_length() - 1
    rows = qa.shape[2]
    spec = pl.BlockSpec((1, 1, rows, LANES), lambda h, k: (h, k, 0, 0))
    pairs = heads * blocks * rows * 1400
    return pl.pallas_call(
        functools.partial(back_near_kernel, local_rings),
        grid=(heads, blocks),
        in_specs=[
            spec,
            pl.BlockSpec((1, 1, SEGMENT_TILES, LANES), lambda h, k: (h, k, 0, 0)),
            pl.BlockSpec((1, blocks, SEGMENT_TILES, LANES), lambda h, k: (h, 0, 0, 0)),
            pl.BlockSpec((1, 1) + bias.shape[2:], lambda h, k: (h, k, 0, 0)),
        ],
        out_specs=[spec, pl.BlockSpec((1, blocks, LANES, SEGMENT_TILES), lambda h, k: (h, 0, 0, 0))],
        out_shape=[
            jax.ShapeDtypeStruct((heads, blocks, rows, LANES), F32),
            jax.ShapeDtypeStruct((heads, blocks, LANES, SEGMENT_TILES), F32),
        ],
        cost_estimate=pl.CostEstimate(
            flops=pairs * 2560, bytes_accessed=heads * blocks * rows * 2500, transcendentals=pairs
        ),
        compiler_params=pltpu.CompilerParams(vmem_limit_bytes=VMEM_LIMIT),
        name="back_near",
    )(qa, do, kv, bias)


def back_far_kernel(
    local_rings, blocks, qa_ref, do_ref, kv_ref, far_ref, bias_ref, dq_ref, dkv_ref, dfar_ref
):
    rows = SEGMENT_TILES >> (local_rings + 1)
    groups = far_groups(local_rings)
    dq_ref[...] = jnp.zeros_like(dq_ref)
    for piece in far_score_list(local_rings, blocks, qa_ref, kv_ref, far_ref):
        ring, block, other, prefix, count, place = piece
        q = far_left(piece, qa_ref, blocks)
        grad = far_left(piece, do_ref, blocks)
        kv = far_keys(piece, kv_ref, far_ref, local_rings)
        raw = dot(q, kv, 1, 1)
        owners = [block] if block is not None else range(blocks)
        parts = [
            add_bias(raw[at * count : (at + 1) * count], bias_ref, one, place, groups, count)
            for at, one in enumerate(owners)
        ]
        scores = parts[0] if len(parts) == 1 else jnp.concatenate(parts, axis=0)
        weights = jnp.exp2(scores)
        grads = (weights * dot(grad, kv, 1, 1)).astype(BF16)
        dq = dot(grads, kv, 1, 0)
        for at, one in enumerate(owners):
            dq_ref[0, one, :count, :] += dq[at * count : (at + 1) * count]
        dkv = dot(q.T, grads, 1, 0) + dot(grad.T, weights.astype(BF16), 1, 0)
        if block is None:
            start = (ring - local_rings - 1) * RING_KEYS
            dfar_ref[0, start : start + RING_KEYS, :] = dkv.T.astype(BF16)
        elif ring == 0:
            dkv_ref[0, other] = dkv
        else:
            dkv_ref[0, other, :, :prefix] += dkv


def back_far(qa, do, kv, far, bias):
    heads, blocks = kv.shape[:2]
    local_rings = blocks.bit_length() - 1
    rows = SEGMENT_TILES >> (local_rings + 1)
    whole = lambda shape: pl.BlockSpec((1,) + shape[1:], lambda h: (h,) + (0,) * (len(shape) - 1))
    pairs = heads * blocks * rows * 2600
    turned = (heads, blocks, LANES, SEGMENT_TILES)
    return pl.pallas_call(
        functools.partial(back_far_kernel, local_rings, blocks),
        grid=(heads,),
        in_specs=[
            whole(qa.shape),
            pl.BlockSpec((1, blocks, rows, LANES), lambda h: (h, 0, 0, 0)),
            whole(kv.shape),
            whole(far.shape),
            whole(bias.shape),
        ],
        out_specs=[whole(qa.shape), whole(turned), whole(far.shape)],
        out_shape=[
            jax.ShapeDtypeStruct(qa.shape, F32),
            jax.ShapeDtypeStruct(turned, F32),
            jax.ShapeDtypeStruct(far.shape, BF16),
        ],
        cost_estimate=pl.CostEstimate(
            flops=pairs * 2560, bytes_accessed=heads * 6 * 1024 * 1024, transcendentals=pairs
        ),
        compiler_params=pltpu.CompilerParams(vmem_limit_bytes=VMEM_LIMIT),
        name="back_far",
    )(qa, do, kv, far, bias)


def narrow(heads):
    local_width = heads * HEAD_WIDTH
    table = np.zeros((heads, 2 * LANES, 3 * local_width), np.float32)
    column = np.arange(HEAD_WIDTH)
    for head in range(heads):
        start = head * HEAD_WIDTH + column
        table[head, column, start] = 1
        table[head, LANES + column, local_width + start] = 1
        table[head, LANES + HEAD_WIDTH + column, 2 * local_width + start] = 1
    return table.reshape(heads * 2 * LANES, 3 * local_width)


def collect_kernel(heads, row_count, counts, score_scale, base_ref, *refs):
    dq_far_ref, dq_near_ref, one_ref, two_ref = refs[:4]
    returned = refs[4 : 4 + len(counts)]
    place_ref, out_ref, held_ref, wide_ref = refs[4 + len(counts) :]
    piece = row_count // RESIDUES
    halves = SEGMENT_TILES // row_count
    far_rows = dq_far_ref.shape[2]
    for head in range(heads):
        held_ref[...] = (one_ref[head, 0] + two_ref[head, 0]).T
        for back_ref, count in zip(returned, counts):
            held_ref[:count, :] += back_ref[head, 0].astype(F32)
        lane = lax.broadcasted_iota(jnp.int32, (piece, LANES), 1)
        factor = jnp.where(lane < HEAD_WIDTH, LN2, jnp.where(lane < SUM_LANE, 1.0, 0.0))
        q_factor = jnp.where(lane < HEAD_WIDTH, score_scale, 0.0)
        for slab in range(RESIDUES):
            residue = lax.rem(base_ref[0] + head + ORDER[slab], RESIDUES)
            for half in range(halves):
                start = slab * SLAB + half * piece
                if start < far_rows:
                    value = dq_far_ref[head, 0, start : start + piece, :]
                else:
                    value = dq_near_ref[head, 0, start - far_rows : start - far_rows + piece, :]
                target = pl.ds(pl.multiple_of(half * row_count + residue * piece, piece), piece)
                at = head * 2 * LANES
                wide_ref[target, at : at + LANES] = (value * q_factor).astype(BF16)
                wide_ref[target, at + LANES : at + 2 * LANES] = (
                    held_ref[start : start + piece, :] * factor
                ).astype(BF16)
    out_ref[...] = dot(wide_ref[...], place_ref[...], 1, 0).astype(BF16)


def collect(base, dq_far, dq_near, dkv_one, dkv_two, returned, row_count, score_scale):
    heads, blocks = dq_far.shape[:2]
    counts = tuple(one.shape[2] for one in returned)
    part = lambda shape: pl.BlockSpec((heads, 1) + shape[2:], lambda k, *_: (0, k, 0, 0))
    arrays = (dq_far, dq_near, dkv_one, dkv_two) + tuple(returned)
    place = jnp.asarray(narrow(heads), BF16)
    wide, width = place.shape
    return pl.pallas_call(
        functools.partial(collect_kernel, heads, row_count, counts, score_scale),
        grid_spec=pltpu.PrefetchScalarGridSpec(
            num_scalar_prefetch=1,
            grid=(blocks,),
            in_specs=[part(one.shape) for one in arrays]
            + [pl.BlockSpec(place.shape, lambda k, *_: (0, 0))],
            out_specs=pl.BlockSpec((SEGMENT_TILES, width), lambda k, *_: (k, 0)),
            scratch_shapes=[
                pltpu.VMEM((SEGMENT_TILES, LANES), F32),
                pltpu.VMEM((SEGMENT_TILES, wide), BF16),
            ],
        ),
        out_shape=jax.ShapeDtypeStruct((blocks * SEGMENT_TILES, width), BF16),
        cost_estimate=pl.CostEstimate(
            flops=2 * blocks * SEGMENT_TILES * wide * width,
            bytes_accessed=blocks * SEGMENT_TILES * wide * 10,
            transcendentals=0,
        ),
        compiler_params=pltpu.CompilerParams(vmem_limit_bytes=VMEM_LIMIT),
        name="collect",
    )(base, *arrays, place)


def partner(index, flip):
    bit = 1
    while bit <= flip:
        if flip & bit:
            index = index + bit - 2 * bit * lax.rem(lax.div(index, bit), 2)
        bit *= 2
    return index


def greet(partners):
    barrier = pltpu.get_barrier_semaphore()
    for device in partners:
        pl.semaphore_signal(barrier, inc=1, device_id=device, device_id_type=MESH)
    pl.semaphore_wait(barrier, len(partners))


def exchange_kernel(count, x_ref, out_ref, send_sem, recv_sem, local_sem):
    rank = lax.axis_index("head")
    greet([{"head": partner(rank, flip)} for flip in range(1, count)])
    keep = pltpu.make_async_copy(x_ref.at[rank], out_ref.at[0], local_sem)
    keep.start()
    copies = []
    for flip in range(1, count):
        to = partner(rank, flip)
        copies.append(
            pltpu.make_async_remote_copy(
                src_ref=x_ref.at[to],
                dst_ref=out_ref.at[flip],
                send_sem=send_sem.at[flip - 1],
                recv_sem=recv_sem.at[flip - 1],
                device_id={"head": to},
                device_id_type=MESH,
            )
        )
        copies[-1].start()
    for copy in copies:
        copy.wait()
    keep.wait()


def exchange_back_kernel(count, x_ref, out_ref, send_sem, recv_sem, local_sem):
    rank = lax.axis_index("head")
    greet([{"head": partner(rank, flip)} for flip in range(1, count)])
    keep = pltpu.make_async_copy(x_ref.at[0], out_ref.at[rank], local_sem)
    keep.start()
    copies = []
    for flip in range(1, count):
        copies.append(
            pltpu.make_async_remote_copy(
                src_ref=x_ref.at[flip],
                dst_ref=out_ref.at[rank],
                send_sem=send_sem.at[flip - 1],
                recv_sem=recv_sem.at[flip - 1],
                device_id={"head": partner(rank, flip)},
                device_id_type=MESH,
            )
        )
        copies[-1].start()
    for copy in copies:
        copy.wait()
    keep.wait()


def exchange_rows(parts, collective_id):
    return exchange_call(exchange_kernel, parts, collective_id)


def exchange_back(parts, collective_id):
    return exchange_call(exchange_back_kernel, parts, collective_id)


def exchange_call(kernel, parts, collective_id):
    count = parts.shape[0]
    return pl.pallas_call(
        functools.partial(kernel, count),
        in_specs=[pl.BlockSpec(memory_space=pltpu.VMEM)],
        out_specs=pl.BlockSpec(memory_space=pltpu.VMEM),
        out_shape=jax.ShapeDtypeStruct(parts.shape, parts.dtype),
        scratch_shapes=[
            pltpu.SemaphoreType.DMA((count - 1,)),
            pltpu.SemaphoreType.DMA((count - 1,)),
            pltpu.SemaphoreType.DMA,
        ],
        compiler_params=pltpu.CompilerParams(
            collective_id=collective_id, has_side_effects=True, vmem_limit_bytes=VMEM_LIMIT
        ),
        name="exchange_rows",
    )(parts)


def gather_kernel(x_ref, out_ref, send_sem, recv_sem, local_sem):
    rank = lax.axis_index("head")
    side, across = partner(rank, 1), partner(rank, 2)
    greet([{"head": side}, {"head": across}])
    half = x_ref.shape[0] // 2
    first, second = pl.ds(0, half), pl.ds(half, half)
    keep = pltpu.make_async_copy(x_ref, out_ref.at[rank], local_sem)
    keep.start()

    def send(step, source, owner, part, to):
        copy = pltpu.make_async_remote_copy(
            src_ref=source.at[part],
            dst_ref=out_ref.at[owner, part],
            send_sem=send_sem.at[step],
            recv_sem=recv_sem.at[step],
            device_id={"head": to},
            device_id_type=MESH,
        )
        copy.start()
        return copy

    copies = [
        send(0, x_ref, rank, first, side),
        send(1, x_ref, rank, second, across),
        send(2, x_ref, rank, second, side),
        send(3, x_ref, rank, first, across),
    ]
    copies[0].wait_recv()
    copies.append(send(4, out_ref.at[side], side, first, across))
    copies[1].wait_recv()
    copies.append(send(5, out_ref.at[across], across, second, side))
    for copy in copies[2:]:
        copy.wait_recv()
    for copy in copies:
        copy.wait_send()
    keep.wait()


def gather_rows(rows, collective_id):
    count, width = rows.shape
    return pl.pallas_call(
        gather_kernel,
        in_specs=[pl.BlockSpec(memory_space=pltpu.VMEM)],
        out_specs=pl.BlockSpec(memory_space=pltpu.VMEM),
        out_shape=jax.ShapeDtypeStruct((4, count, width), rows.dtype),
        scratch_shapes=[
            pltpu.SemaphoreType.DMA((6,)),
            pltpu.SemaphoreType.DMA((6,)),
            pltpu.SemaphoreType.DMA,
        ],
        compiler_params=pltpu.CompilerParams(
            collective_id=collective_id, has_side_effects=True, vmem_limit_bytes=VMEM_LIMIT
        ),
        name="gather_rows",
    )(rows).reshape(4 * count, width)


def as_two(value):
    high = value.astype(BF16)
    return high, (value - high.astype(F32)).astype(BF16)


def finale_kernel(
    proj_ref,
    x_ref,
    w_ref,
    small_ref,
    gain_ref,
    shift_ref,
    hat_ref,
    inv_ref,
    res_ref,
    grad_ref,
    weight_ref,
    total_ref,
    column_ref,
    out_buf,
    own_buf,
    side_buf,
    across_buf,
    corner_buf,
    dw_buf,
    dw_send,
    dw_recv,
    dw_half,
    dw_quarter,
    dw_all,
    small_buf,
    small_recv,
    both_buf,
    both_recv,
    send_sem,
    recv_sem,
):
    rank, pair, core = lax.axis_index("head"), lax.axis_index("pair"), lax.axis_index("core")
    side, across, corner = partner(rank, 1), partner(rank, 2), partner(rank, 3)
    other_core = {"core": 1 - core}
    pairs = [{"pair": partner(pair, flip)} for flip in (1, 2, 3)]
    heads = [{"head": side}, {"head": across}, {"head": corner}]
    greet(heads + pairs + [other_core])
    rows = grad_ref.shape[0]
    half = rows // 2
    first, second = pl.ds(0, half), pl.ds(half, half)
    started = []

    def send(source, target, device):
        step = len(started)
        copy = pltpu.make_async_remote_copy(
            src_ref=source,
            dst_ref=target,
            send_sem=send_sem.at[step],
            recv_sem=recv_sem.at[step],
            device_id=device,
            device_id_type=MESH,
        )
        copy.start()
        started.append(copy)
        return copy

    def share(member):
        piece = proj_ref[pl.ds(pl.multiple_of(member * rows, rows), rows), :]
        return dot(piece, w_ref[...], 1, 1)

    out_buf[2] = share(corner).astype(BF16)
    via_side = send(out_buf.at[2, first], corner_buf.at[0], heads[0])
    via_across = send(out_buf.at[2, second], corner_buf.at[1], heads[1])
    out_buf[0] = share(side).astype(BF16)
    side_first = send(out_buf.at[0, first], side_buf.at[first], heads[0])
    out_buf[1] = share(across).astype(BF16)
    across_second = send(out_buf.at[1, second], across_buf.at[second], heads[1])

    dw_buf[...] = dot(x_ref[...], proj_ref[...], 0, 0)
    depth = dw_send.shape[0]
    dw_send[...] = dw_buf[pl.ds(pl.multiple_of((1 - core) * depth, depth), depth), :].astype(BF16)
    halves = send(dw_send, dw_recv, other_core)
    columns = dot(jnp.ones((8, proj_ref.shape[0]), BF16), proj_ref[...], 1, 0)
    shift_sum = sum(dot(part, w_ref[...], 1, 1) for part in as_two(columns))
    ones = jnp.ones((8, w_ref.shape[1]), BF16)
    product = w_ref[...].astype(F32) * dw_buf[...]
    gain_sum = sum(dot(ones, part, 1, 1) for part in as_two(product))
    gain_sum = (gain_sum - shift_ref[...] * shift_sum) / gain_ref[...]
    line = lax.broadcasted_iota(jnp.int32, gain_sum.shape, 0)
    small_buf[...] = jnp.where(line == 4, gain_sum, jnp.where(line == 5, shift_sum, small_ref[...]))
    small = [send(small_buf, small_recv.at[step], heads[step]) for step in range(3)]
    own_buf[...] = share(rank)

    via_side.wait_recv()
    out_buf[1, first, :] = (out_buf[1, first, :].astype(F32) + corner_buf[0].astype(F32)).astype(BF16)
    across_first = send(out_buf.at[1, first], across_buf.at[first], heads[1])
    via_across.wait_recv()
    out_buf[0, second, :] = (
        out_buf[0, second, :].astype(F32) + corner_buf[1].astype(F32)
    ).astype(BF16)
    side_second = send(out_buf.at[0, second], side_buf.at[second], heads[0])

    halves.wait_recv()
    dw_half[...] = (
        dw_buf[pl.ds(pl.multiple_of(core * depth, depth), depth), :] + dw_recv[...].astype(F32)
    ).astype(BF16)
    slim = depth // 4
    quarter = lambda member: pl.ds(pl.multiple_of(member * slim, slim), slim)
    quarters = [
        send(dw_half.at[quarter(device["pair"])], dw_quarter.at[step], device)
        for step, device in enumerate(pairs)
    ]
    for copy in small:
        copy.wait_recv()
    both_buf[0, :8, :] = small_buf[...] + small_recv[0] + small_recv[1] + small_recv[2]
    wide = columns.shape[1]
    both_buf[0, 8:, :] = jnp.zeros_like(both_buf[0, 8:, :])
    both_buf[0, 8:, :wide] = columns
    small_core = send(both_buf.at[0], both_recv.at[0], other_core)
    small_core.wait_recv()
    both_buf[1] = both_buf[0] + both_recv[0]
    small_pairs = [
        send(both_buf.at[1], both_recv.at[1 + step], device) for step, device in enumerate(pairs)
    ]

    for copy in quarters:
        copy.wait_recv()
    dw_all[core, pair] = (
        dw_half[quarter(pair), :].astype(F32)
        + dw_quarter[0].astype(F32)
        + dw_quarter[1].astype(F32)
        + dw_quarter[2].astype(F32)
    ).astype(BF16)
    back = [send(dw_all.at[core, pair], dw_all.at[core, pair], device) for device in pairs]
    for copy in small_pairs:
        copy.wait_recv()
    total = both_buf[1] + both_recv[1] + both_recv[2] + both_recv[3]
    total_ref[...] = total[:8]
    column_ref[...] = total[8:, :wide]
    for copy in back:
        copy.wait_recv()
    last = send(dw_all.at[core], dw_all.at[core], other_core)

    for copy in (side_first, side_second, across_first, across_second):
        copy.wait_recv()
    grad = own_buf[...] + side_buf[...].astype(F32) + across_buf[...].astype(F32)
    scaled = grad * gain_ref[...]
    hat = hat_ref[...]
    grad_ref[...] = res_ref[...] + inv_ref[...] * (
        scaled
        - jnp.mean(scaled, axis=1, keepdims=True)
        - hat * jnp.mean(scaled * hat, axis=1, keepdims=True)
    )
    last.wait_recv()
    weight_ref[...] = dw_all[...].reshape(weight_ref.shape).astype(F32)
    for copy in started:
        copy.wait_send()


def finale(proj, rows, weight, small, gain, shift, hat, inverse, residual, collective_id):
    count, width = hat.shape
    columns = proj.shape[1]
    depth = width // 2
    steps = 24
    vmem = pl.BlockSpec(memory_space=pltpu.VMEM)
    return pl.pallas_call(
        finale_kernel,
        in_specs=[vmem] * 9,
        out_specs=[vmem] * 4,
        out_shape=[
            jax.ShapeDtypeStruct((count, width), F32),
            jax.ShapeDtypeStruct((width, columns), F32),
            jax.ShapeDtypeStruct((8, width), F32),
            jax.ShapeDtypeStruct((8, columns), F32),
        ],
        scratch_shapes=[
            pltpu.VMEM((3, count, width), BF16),
            pltpu.VMEM((count, width), F32),
            pltpu.VMEM((count, width), BF16),
            pltpu.VMEM((count, width), BF16),
            pltpu.VMEM((2, count // 2, width), BF16),
            pltpu.VMEM((width, columns), F32),
            pltpu.VMEM((depth, columns), BF16),
            pltpu.VMEM((depth, columns), BF16),
            pltpu.VMEM((depth, columns), BF16),
            pltpu.VMEM((3, depth // 4, columns), BF16),
            pltpu.VMEM((2, 4, depth // 4, columns), BF16),
            pltpu.VMEM((8, width), F32),
            pltpu.VMEM((3, 8, width), F32),
            pltpu.VMEM((2, 16, width), F32),
            pltpu.VMEM((4, 16, width), F32),
            pltpu.SemaphoreType.DMA((steps,)),
            pltpu.SemaphoreType.DMA((steps,)),
        ],
        cost_estimate=pl.CostEstimate(
            flops=4 * proj.shape[0] * width * columns, bytes_accessed=12_000_000, transcendentals=0
        ),
        compiler_params=pltpu.CompilerParams(
            collective_id=collective_id, has_side_effects=True, vmem_limit_bytes=VMEM_LIMIT
        ),
        name="finale",
    )(proj, rows, weight, small, gain, shift, hat, inverse, residual)


def mid_kernel(
    count,
    base_ref,
    attn_ref,
    features_ref,
    cotangent_ref,
    out_ref,
    up_mine_ref,
    down_mine_ref,
    up_other_ref,
    down_other_ref,
    up_bias_ref,
    rows_ref,
    table_ref,
    result_ref,
    up_keep_ref,
    down_keep_ref,
    up_give_ref,
    down_give_ref,
    out_keep_ref,
    out_give_ref,
    bias_ref,
    back_ref,
    grad_ref,
    small_ref,
    residual_buf,
    hat_buf,
    inverse_buf,
    normed_buf,
    total_buf,
    grad_buf,
    up_buf,
    down_buf,
    attn_buf,
):
    step = pl.program_id(0)
    core = base_ref[1]
    local_width = table_ref.shape[1]
    out_bias, mlp_gain, mlp_shift, down_bias = [rows_ref[k : k + 1, :] for k in range(4)]

    @pl.when(step == 0)
    def _():
        half = attn_ref.shape[1]
        total = features_ref[...].astype(F32) + out_bias
        for part in range(count):
            for side in range(2):
                attn_buf[part, side * half : (side + 1) * half, :] = dot(
                    attn_ref[part], table_ref[side], 1, 1
                ).astype(BF16)
            weight = out_ref[part * local_width : (part + 1) * local_width, :]
            total = total + dot(attn_buf[part], weight, 1, 0)
        residual_buf[...] = total
        center = total - jnp.mean(total, axis=1, keepdims=True)
        inverse = lax.rsqrt(jnp.mean(center * center, axis=1, keepdims=True) + epsilon)
        hat = center * inverse
        hat_buf[...] = hat
        inverse_buf[...] = jnp.broadcast_to(inverse, inverse_buf.shape)
        normed_buf[...] = (hat * mlp_gain + mlp_shift).astype(BF16)
        total_buf[...] = jnp.zeros_like(total_buf)
        grad_buf[...] = jnp.zeros_like(grad_buf)

    half_of = lambda ref, place: pl.ds(
        pl.multiple_of(place * (ref.shape[0] // 2), ref.shape[0] // 2), ref.shape[0] // 2
    )
    for up_ref, down_ref, place in (
        (up_mine_ref, down_mine_ref, core),
        (up_other_ref, down_other_ref, 1 - core),
    ):
        up_buf[half_of(up_buf, place), :] = up_ref[0, 0]
        down_buf[half_of(down_buf, place), :] = down_ref[0, 0]
    normed, cotangent = normed_buf[...], cotangent_ref[...]
    value = dot(normed, up_buf[...], 1, 0) + up_bias_ref[0]
    square = value * value
    factor = math.sqrt(2.0 / math.pi)
    bent = jnp.tanh(factor * value * (1.0 + 0.044715 * square))
    share = 0.5 * (1.0 + bent)
    hidden = (value * share).astype(BF16)
    slope = share + 0.5 * value * (1.0 - bent * bent) * (factor * (1.0 + 3 * 0.044715 * square))
    total_buf[...] += dot(hidden, down_buf[...], 1, 0)
    grad_pre = (dot(cotangent, down_buf[...], 1, 1) * slope).astype(BF16)
    bias_ref[0] = jnp.sum(grad_pre.astype(F32), axis=0, keepdims=True)
    grad_buf[...] += dot(grad_pre, up_buf[...], 1, 1)
    up_buf[...] = dot(normed, grad_pre, 0, 0).astype(BF16)
    down_buf[...] = dot(hidden, cotangent, 0, 0).astype(BF16)
    for up_ref, down_ref, place in (
        (up_keep_ref, down_keep_ref, core),
        (up_give_ref, down_give_ref, 1 - core),
    ):
        up_ref[0] = up_buf[half_of(up_buf, place), :]
        down_ref[0] = down_buf[half_of(down_buf, place), :]

    @pl.when(step == count - 1)
    def _():
        result_ref[...] = (residual_buf[...] + total_buf[...] + down_bias).astype(BF16)
        cotangent32 = cotangent_ref[...].astype(F32)
        hat = hat_buf[...]
        grad = grad_buf[...]
        scaled = grad * mlp_gain
        inverse = inverse_buf[:, :1]
        full = cotangent32 + inverse * (
            scaled
            - jnp.mean(scaled, axis=1, keepdims=True)
            - hat * jnp.mean(scaled * hat, axis=1, keepdims=True)
        )
        grad_ref[...] = full
        sums = [
            jnp.sum(grad * hat, axis=0, keepdims=True),
            jnp.sum(grad, axis=0, keepdims=True),
            jnp.sum(full, axis=0, keepdims=True),
            jnp.sum(cotangent32, axis=0, keepdims=True),
        ]
        small_ref[...] = jnp.concatenate(sums + [jnp.zeros((4, full.shape[1]), F32)], axis=0)
        low = full.astype(BF16)
        slim = local_width // 2
        for part in range(count):
            weight = out_ref[part * local_width : (part + 1) * local_width, :]
            back = dot(low, weight, 1, 1).astype(BF16)
            back_ref[part] = side_by_side(back, table_ref).astype(BF16)
            grad_out = dot(attn_buf[part], low, 0, 0)
            total_buf[:local_width, :] = grad_out
            for ref, place in ((out_keep_ref, core), (out_give_ref, 1 - core)):
                ref[part] = total_buf[pl.ds(pl.multiple_of(place * slim, slim), slim), :].astype(BF16)


def mid(base, attn, features, cotangent, out_all, mine, other, up_bias, rows):
    count = attn.shape[0]
    row_count, width = features.shape
    local_width = attn.shape[2] // 2
    table = jnp.asarray(pair_placement(local_width), BF16)
    hidden = up_bias.shape[2]
    weight = lambda arrays, k: pl.BlockSpec(
        (1, 1) + arrays[min(k, len(arrays) - 1)].shape[2:],
        lambda step, *_: (step, k if len(arrays) == 1 else 0, 0, 0),
    )
    whole = lambda x: pl.BlockSpec(x.shape, lambda k, *_: (0,) * len(x.shape))
    step = lambda shape: pl.BlockSpec((1,) + shape[1:], lambda k, *_: (k,) + (0,) * (len(shape) - 1))
    outs = [
        jax.ShapeDtypeStruct((row_count, width), BF16),
        jax.ShapeDtypeStruct((count, width // 2, hidden), BF16),
        jax.ShapeDtypeStruct((count, hidden // 2, width), BF16),
        jax.ShapeDtypeStruct((count, width // 2, hidden), BF16),
        jax.ShapeDtypeStruct((count, hidden // 2, width), BF16),
        jax.ShapeDtypeStruct((count, local_width // 2, width), BF16),
        jax.ShapeDtypeStruct((count, local_width // 2, width), BF16),
        jax.ShapeDtypeStruct((count, 1, hidden), F32),
        jax.ShapeDtypeStruct(attn.shape, BF16),
        jax.ShapeDtypeStruct((row_count, width), F32),
        jax.ShapeDtypeStruct((8, width), F32),
    ]
    stepped = (1, 2, 3, 4, 7)
    return pl.pallas_call(
        functools.partial(mid_kernel, count),
        grid_spec=pltpu.PrefetchScalarGridSpec(
            num_scalar_prefetch=1,
            grid=(count,),
            in_specs=[
                whole(attn),
                whole(features),
                whole(cotangent),
                whole(out_all),
                weight(mine, 0),
                weight(mine, 1),
                weight(other, 0),
                weight(other, 1),
                step(up_bias.shape),
                whole(rows),
                whole(table),
            ],
            out_specs=[step(o.shape) if k in stepped else whole(o) for k, o in enumerate(outs)],
            scratch_shapes=[
                pltpu.VMEM((row_count, width), F32),
                pltpu.VMEM((row_count, width), F32),
                pltpu.VMEM((row_count, LANES), F32),
                pltpu.VMEM((row_count, width), BF16),
                pltpu.VMEM((row_count, width), F32),
                pltpu.VMEM((row_count, width), F32),
                pltpu.VMEM((width, hidden), BF16),
                pltpu.VMEM((hidden, width), BF16),
                pltpu.VMEM((count, row_count, local_width), BF16),
            ],
        ),
        out_shape=outs,
        cost_estimate=pl.CostEstimate(
            flops=12 * row_count * width * hidden * count,
            bytes_accessed=30_000_000,
            transcendentals=row_count * hidden * count,
        ),
        compiler_params=pltpu.CompilerParams(vmem_limit_bytes=VMEM_LIMIT),
        name="mid",
    )(
        base,
        attn,
        features,
        cotangent,
        out_all,
        mine[0],
        mine[-1],
        other[0],
        other[-1],
        up_bias,
        rows,
        table,
    )


def residue_major(rows):
    count, width = rows.shape
    return rows.reshape(count // RESIDUES, RESIDUES, width).swapaxes(0, 1).reshape(count, width)


def position_major(rows):
    count, width = rows.shape
    return rows.reshape(RESIDUES, count // RESIDUES, width).swapaxes(0, 1).reshape(count, width)


def norm_forward(values, norm_gain, norm_shift):
    center = values - jnp.mean(values, axis=-1, keepdims=True)
    inverse = lax.rsqrt(jnp.mean(center * center, axis=-1, keepdims=True) + epsilon)
    normed = center * inverse
    return (normed * norm_gain + norm_shift, normed, inverse)


def norm_backward(grad_out, normed, inverse, norm_gain):
    scaled = grad_out * norm_gain
    return inverse * (
        scaled
        - jnp.mean(scaled, axis=-1, keepdims=True)
        - normed * jnp.mean(scaled * normed, axis=-1, keepdims=True)
    )


def gelu_tanh(values):
    return jax.nn.gelu(values, approximate=True)


def from_other(x, axis, flip):
    return lax.ppermute(x, axis, [(i, i ^ flip) for i in range(lax.axis_size(axis))])


def per_device(
    tile_features,
    slide_lengths,
    qkv_weight,
    qv_bias,
    out_weight,
    out_bias,
    attn_gain,
    attn_shift,
    mlp_gain,
    mlp_shift,
    up_weight,
    up_bias,
    down_weight,
    down_bias,
    output_cotangent,
):
    row_count = tile_features.shape[2]
    width = tile_features.shape[3]
    local_width = qkv_weight.shape[2]
    heads = local_width // HEAD_WIDTH
    sequence_member = lax.axis_index(SEQ)
    head_rank = lax.axis_index("head")
    head_count = lax.axis_size("head")
    extent = row_count * head_count
    blocks = extent // SEGMENT_TILES
    local_rings = blocks.bit_length() - 1
    score_scale = HEAD_WIDTH ** (-0.5)
    query_scale = score_scale / LN2
    core = lax.axis_index("core")
    base = jnp.stack([head_rank * heads, core]).astype(jnp.int32)

    own_rows = residue_major(tile_features.reshape(row_count, width))
    features = own_rows.astype(F32)
    normed_one, hat_one, inv_one = norm_forward(features, attn_gain, attn_shift)
    normed_one = normed_one.astype(BF16)
    pair_count = lax.axis_size("pair")
    square = head_count == 4 and pair_count == 4
    if head_count == 4:
        gathered_one = gather_rows(normed_one, 0)
    else:
        gathered_one = lax.all_gather(normed_one, "head", axis=0, tiled=True)

    by_head = qkv_weight.reshape(width, 3, heads, HEAD_WIDTH)
    query_weight = jnp.pad(by_head[:, 0], ((0, 0), (0, 0), (0, LANES - HEAD_WIDTH)))
    pair_weight = jnp.pad(
        jnp.concatenate([by_head[:, 1], by_head[:, 2]], axis=-1),
        ((0, 0), (0, 0), (0, LANES - 2 * HEAD_WIDTH)),
    )
    wide = jnp.concatenate([query_weight, pair_weight], axis=-1).reshape(width, heads * 2 * LANES)
    scale_row = np.ones((heads, 2 * LANES), np.float32)
    scale_row[:, :HEAD_WIDTH] = query_scale
    by_head_bias = qv_bias.reshape(2, heads, HEAD_WIDTH)
    ones = np.zeros((heads, LANES - 2 * HEAD_WIDTH), np.float32)
    ones[:, : 1 + AUX_COUNT] = 1.0
    wide_bias = jnp.concatenate(
        [
            by_head_bias[0],
            jnp.zeros((heads, LANES - HEAD_WIDTH), F32),
            jnp.zeros((heads, HEAD_WIDTH), F32),
            by_head_bias[1],
            jnp.asarray(ones),
        ],
        axis=1,
    ).reshape(1, heads * 2 * LANES)
    scale_row = jnp.asarray(scale_row).reshape(1, heads * 2 * LANES)
    bias = key_bias(slide_lengths, sequence_member, head_rank * heads, heads, blocks, row_count)

    hidden_local = up_weight.shape[1]
    bias_rows = jnp.zeros((RESIDUES, width), F32)
    for step, one in enumerate(split_exact(up_bias)):
        bias_rows = bias_rows.at[step, :hidden_local].set(one)
    out_rows = jnp.concatenate([out_weight, bias_rows.astype(BF16)], axis=0)
    up_half = lax.dynamic_slice_in_dim(up_weight, core * (width // 2), width // 2, 0)
    down_half = lax.dynamic_slice_in_dim(down_weight, core * (hidden_local // 2), hidden_local // 2, 0)
    joined = up_half.shape == down_half.shape
    mine = (jnp.stack([up_half, down_half]),) if joined else (up_half[None], down_half[None])
    out_rows, mine, gathered_one = lax.optimization_barrier((out_rows, mine, gathered_one))
    mine = tuple(lax.all_gather(one, "head", axis=0) for one in mine)
    turned = [out_rows] + [from_other(out_rows, "head", flip) for flip in range(1, head_count)]
    out_all = jnp.concatenate([one[:local_width] for one in turned], axis=0)
    ranks = head_rank ^ jnp.arange(head_count)
    up_bias_all = jnp.stack(
        [jnp.sum(one[local_width : local_width + 3, :hidden_local].astype(F32), axis=0) for one in turned]
    )[ranks]
    q, kv = project(
        base, gathered_one, wide, jnp.concatenate([wide_bias, scale_row], axis=0), heads, row_count
    )
    received = []
    for ring in range(local_rings + 1, LEVELS):
        prefix = SEGMENT_TILES >> ring
        sent = kv[:, :, :prefix].reshape(heads, blocks * prefix, LANES)
        for flip in ring_members(ring, blocks):
            received.append(from_other(sent, SEQ, flip))
    o_near, qa_near = attend_near(q, kv, bias)
    far = jnp.concatenate(received, axis=1)
    o_far, qa_far = attend_far(q, kv, far, bias)
    packed = pack(base, o_far, o_near, row_count)
    mine, packed = lax.optimization_barrier((mine, packed))
    other = tuple(from_other(one, "core", 1) for one in mine)
    attn_parts = exchange_rows(packed, 1)
    cotangent = residue_major(output_cotangent.reshape(row_count, width))
    rows = jnp.stack([out_bias, mlp_gain, mlp_shift, down_bias])
    output, up_keep, down_keep, up_give, down_give, out_keep, out_give, bias_sums, back, grad_residual, small = mid(
        base,
        attn_parts,
        own_rows,
        cotangent,
        out_all,
        mine,
        other,
        up_bias_all[:, None],
        jnp.pad(rows, ((0, 4), (0, 0))),
    )
    output = position_major(output).reshape(tile_features.shape)
    grad_parts = exchange_back(back, 2)

    do = unpack(base, grad_parts, o_far, o_near, row_count)
    dq_far, dkv_far, dfar = back_far(qa_far, do, kv, far, bias)
    returned = []
    at = 0
    for ring in range(local_rings + 1, LEVELS):
        prefix = SEGMENT_TILES >> ring
        for flip in ring_members(ring, blocks):
            sent = dfar[:, at : at + blocks * prefix]
            at += blocks * prefix
            returned.append(
                from_other(sent, SEQ, flip).reshape(heads, blocks, prefix, LANES)
            )
    dq_near, dkv_near = back_near(qa_near, do, kv, bias)

    scatter = lambda x: lax.psum_scatter(x, "head", scatter_dimension=0, tiled=True)

    rows_of = lambda x: x.reshape(head_count, -1, width)
    flat = lambda x, y, z: jnp.concatenate([rows_of(x), rows_of(y), z[ranks]], axis=1)
    bias_rows = jnp.pad(bias_sums, ((0, 0), (0, RESIDUES - 1), (0, width - hidden_local)))
    given = from_other(flat(up_give, down_give, out_give), "core", 1)
    own = flat(up_keep, down_keep, out_keep)
    reduced = (own.astype(F32) + given.astype(F32)).astype(BF16)
    reduced = jnp.concatenate([reduced, bias_rows.astype(BF16)], axis=1)
    reduced = scatter(reduced.reshape(-1, width))
    reduced = lax.psum(reduced, "pair")

    grad_proj = collect(base, dq_far, dq_near, dkv_far, dkv_near, returned, row_count, score_scale)
    qkv_flat = qkv_weight.reshape(width, 3 * local_width)
    if square:
        grad_features, grad_qkv, totals, columns = finale(
            grad_proj,
            gathered_one,
            qkv_flat,
            small,
            attn_gain[None],
            attn_shift[None],
            hat_one,
            inv_one,
            grad_residual,
            3,
        )
        columns = columns[0]
    else:
        grad_qkv = dot(gathered_one, grad_proj, 0, 0)
        columns = jnp.sum(grad_proj.astype(F32), axis=0)
        weight32 = qkv_flat.astype(F32)
        shift_sum = jnp.sum(weight32 * columns, axis=1)
        gain_sum = (jnp.sum(weight32 * grad_qkv, axis=1) - attn_shift * shift_sum) / attn_gain
        totals = lax.psum(small.at[4].set(gain_sum).at[5].set(shift_sum), EVERY)
        grad_normed_one = scatter(dot(grad_proj, qkv_flat, 1, 1).astype(BF16)).astype(F32)
        grad_features = grad_residual + norm_backward(grad_normed_one, hat_one, inv_one, attn_gain)
        grad_qkv = lax.psum(grad_qkv.astype(BF16), SEQ).astype(F32)
        columns = lax.psum(columns, SEQ)
    grad_qkv = grad_qkv.reshape(width, 3, local_width)
    grad_qv = jnp.stack([columns[:local_width], columns[2 * local_width :]])
    norm_totals = jnp.stack([totals[4], totals[5], totals[0], totals[1], totals[2], totals[3]])

    reduced, totals = lax.optimization_barrier((reduced, totals))
    given = from_other(reduced, "core", 1)
    low_half = jnp.where(core == 0, reduced, given).astype(F32)
    high_half = jnp.where(core == 0, given, reduced).astype(F32)
    together = lambda a, b: jnp.concatenate([low_half[a:b], high_half[a:b]], axis=0)
    deep = hidden_local // 2
    grad_up = jnp.concatenate(
        [one[:deep].reshape(width // 2, hidden_local) for one in (low_half, high_half)], axis=0
    )
    grad_down = together(deep, 2 * deep)
    after = 2 * deep + local_width // 2
    grad_out = together(2 * deep, after)
    grad_up_bias = low_half[after, :hidden_local] + high_half[after, :hidden_local]
    return (
        output,
        position_major(grad_features).reshape(tile_features.shape),
        grad_qkv,
        grad_qv,
        grad_out,
        norm_totals[4],
        norm_totals[0],
        norm_totals[1],
        norm_totals[2],
        norm_totals[3],
        grad_up,
        grad_up_bias,
        grad_down,
        norm_totals[5],
    )


def solution(mesh):
    in_specs = (
        P(("pair", "core"), "head", None, None),
        P(),
        P(None, None, "head"),
        P(None, "head"),
        P("head", None),
        P(),
        P(),
        P(),
        P(),
        P(),
        P(None, "head"),
        P("head"),
        P("head", None),
        P(),
        P(("pair", "core"), "head", None, None),
    )
    out_specs = (
        P(("pair", "core"), "head", None, None),
        P(("pair", "core"), "head", None, None),
        P(None, None, "head"),
        P(None, "head"),
        P("head", None),
        P(),
        P(),
        P(),
        P(),
        P(),
        P(None, "head"),
        P("head"),
        P("head", None),
        P(),
    )
    split = jax.sharding.Mesh(
        mesh.devices.reshape(mesh.shape["head"], mesh.shape["seq"] // 2, 2), ("head", "pair", "core")
    )
    return jax.shard_map(
        per_device, mesh=split, in_specs=in_specs, out_specs=out_specs, check_vma=False
    )
```

```python
import functools
import math

import jax
import jax.numpy as jnp
import numpy as np
from jax import lax
from jax.experimental import pallas as pl
from jax.experimental.pallas import tpu as pltpu
from jax.sharding import PartitionSpec as P

HEAD_WIDTH = 48
SEGMENT_TILES = 1024
LEVELS = 5
RESIDUES = 16
TAIL_ROWS = 32
LANES = 128
RING_KEYS = SEGMENT_TILES // 2
ORDER = (0, 8, 4, 12, 2, 6, 10, 14, 1, 3, 5, 7, 9, 11, 13, 15)
SLAB = SEGMENT_TILES // RESIDUES

epsilon = 1e-05
masked_low = -1e30
BF16 = jnp.bfloat16
F32 = jnp.float32
MESH = pl.DeviceIdType.MESH
LN2 = math.log(2.0)
SEQ = ("pair", "core")
EVERY = ("head", "pair", "core")
SUM_LANE = 2 * HEAD_WIDTH
AUX_LANE = SUM_LANE + 1
AUX_COUNT = 3
VMEM_LIMIT = 52 * 1024 * 1024


def dot(left_side, right_side, left_dim, right_dim):
    return lax.dot_general(
        left_side,
        right_side,
        (((left_dim,), (right_dim,)), ((), ())),
        preferred_element_type=F32,
    )


def class_rows(level):
    low = SEGMENT_TILES >> (level + 1) if level < LEVELS - 1 else 0
    return low, SEGMENT_TILES >> level


def key_class():
    index = np.arange(SEGMENT_TILES)
    found = np.zeros(SEGMENT_TILES, np.int64)
    for level in range(LEVELS):
        found[index < SEGMENT_TILES >> level] = level
    return found


def multiplicity_table():
    classes = key_class()
    table = np.zeros((LEVELS, SEGMENT_TILES + (LEVELS - 1) * RING_KEYS), np.float32)
    for level in range(LEVELS):
        table[level, :SEGMENT_TILES] = 1 + np.minimum(level, classes)
        for ring in range(1, level + 1):
            prefix = SEGMENT_TILES >> ring
            one = np.minimum(level, classes[:prefix]) - ring + 1
            start = SEGMENT_TILES + (ring - 1) * RING_KEYS
            table[level, start : start + RING_KEYS] = np.tile(one, RING_KEYS // prefix)
    return table


def layout(slide_lengths, positions):
    blocks = (slide_lengths + SEGMENT_TILES - 1) // SEGMENT_TILES
    slide_ends = jnp.cumsum(blocks) * SEGMENT_TILES
    slide_starts = slide_ends - blocks * SEGMENT_TILES
    inside = (positions[..., None] >= slide_starts) & (positions[..., None] < slide_ends)
    labels = jnp.arange(slide_lengths.shape[0], dtype=jnp.int32)
    slide_index = jnp.sum(jnp.where(inside, labels, 0), axis=-1)
    offset = positions - jnp.sum(jnp.where(inside, slide_starts, 0), axis=-1)
    length = jnp.sum(jnp.where(inside, slide_lengths, 0), axis=-1)
    return (slide_index, offset < length)


def ring_members(ring, block_count):
    return range((1 << (ring - 1)) // block_count, (1 << ring) // block_count)


def key_bias(slide_lengths, sequence_member, base_head, heads, block_count, row_count):
    local_rings = block_count.bit_length() - 1
    index = np.arange(SEGMENT_TILES)
    order = np.asarray(ORDER)[index // SLAB]
    piece = row_count // RESIDUES
    spot = (index % SLAB) // piece * row_count + index % piece * RESIDUES
    head = base_head + jnp.arange(heads, dtype=jnp.int32)[:, None]
    inner = spot[None, :] + (head + order[None, :]) % RESIDUES
    first_block = sequence_member * block_count
    per_block = []
    for block in range(block_count):
        parts = [(first_block + block) * SEGMENT_TILES + inner]
        for ring in range(1, LEVELS):
            prefix = SEGMENT_TILES >> ring
            if ring <= local_rings:
                start = (block >> (ring - 1) ^ 1) << (ring - 1)
                ids = [first_block + start + t for t in range(1 << (ring - 1))]
            else:
                ids = [
                    (sequence_member ^ x) * block_count + t
                    for x in ring_members(ring, block_count)
                    for t in range(block_count)
                ]
            parts += [one * SEGMENT_TILES + inner[:, :prefix] for one in ids]
        per_block.append(jnp.concatenate(parts, axis=1))
    positions = jnp.stack(per_block, axis=1).astype(jnp.int32)
    slide, valid = layout(slide_lengths, positions)
    own, _ = layout(
        slide_lengths,
        (first_block + jnp.arange(block_count, dtype=jnp.int32)) * SEGMENT_TILES,
    )
    allowed = (slide == own[None, :, None]) & valid
    table = multiplicity_table()
    logs = np.where(table > 0, np.log2(np.maximum(table, 1)), masked_low).astype(np.float32)
    return jnp.where(allowed[:, :, None, :], logs[None, None], masked_low)


def project_kernel(heads, row_count, base_ref, x_ref, w_ref, b_ref, q_ref, kv_ref, held_ref):
    piece = row_count // RESIDUES
    halves = SEGMENT_TILES // row_count
    for half in range(halves):
        x = x_ref[half * row_count : (half + 1) * row_count, :]
        for head in range(heads):
            columns = slice(head * 2 * LANES, (head + 1) * 2 * LANES)
            wide = dot(x, w_ref[:, columns], 1, 0) + b_ref[0:1, columns]
            held_ref[...] = (wide * b_ref[1:2, columns]).astype(BF16)
            for slab in range(RESIDUES):
                residue = lax.rem(base_ref[0] + head + ORDER[slab], RESIDUES)
                source = pl.ds(pl.multiple_of(residue * piece, piece), piece)
                start = slab * SLAB + half * piece
                q_ref[head, 0, start : start + piece, :] = held_ref[source, :LANES]
                kv_ref[head, 0, start : start + piece, :] = held_ref[source, LANES:]


def project(base, rows, weight, bias, heads, row_count):
    total, width = rows.shape
    blocks = total // SEGMENT_TILES
    shape = jax.ShapeDtypeStruct((heads, blocks, SEGMENT_TILES, LANES), BF16)
    spec = pl.BlockSpec((heads, 1, SEGMENT_TILES, LANES), lambda k, *_: (0, k, 0, 0))
    return pl.pallas_call(
        functools.partial(project_kernel, heads, row_count),
        grid_spec=pltpu.PrefetchScalarGridSpec(
            num_scalar_prefetch=1,
            grid=(blocks,),
            in_specs=[
                pl.BlockSpec((SEGMENT_TILES, width), lambda k, *_: (k, 0)),
                pl.BlockSpec(weight.shape, lambda k, *_: (0, 0)),
                pl.BlockSpec(bias.shape, lambda k, *_: (0, 0)),
            ],
            out_specs=[spec, spec],
            scratch_shapes=[pltpu.VMEM((row_count, 2 * LANES), BF16)],
        ),
        out_shape=[shape, shape],
        cost_estimate=pl.CostEstimate(
            flops=2 * total * width * weight.shape[1], bytes_accessed=8 * total * width, transcendentals=0
        ),
        compiler_params=pltpu.CompilerParams(vmem_limit_bytes=VMEM_LIMIT),
        name="project",
    )(base, rows, weight, bias)


def partner(index, flip):
    bit = 1
    while bit <= flip:
        if flip & bit:
            index = index + bit - 2 * bit * lax.rem(lax.div(index, bit), 2)
        bit *= 2
    return index


def greet(partners):
    barrier = pltpu.get_barrier_semaphore()
    for device in partners:
        pl.semaphore_signal(barrier, inc=1, device_id=device, device_id_type=MESH)
    pl.semaphore_wait(barrier, len(partners))


def sequence_device(flip):
    pair, core = lax.axis_index("pair"), lax.axis_index("core")
    return {"pair": partner(pair, flip // 2), "core": partner(core, flip % 2)}


def ring_flips(blocks):
    local_rings = blocks.bit_length() - 1
    return [
        (ring, place, flip)
        for ring in range(local_rings + 1, LEVELS)
        for place, flip in enumerate(ring_members(ring, blocks))
    ]


def remote(source, target, device, send_sem, recv_sem, step):
    return pltpu.make_async_remote_copy(
        src_ref=source,
        dst_ref=target,
        send_sem=send_sem.at[step],
        recv_sem=recv_sem.at[step],
        device_id=device,
        device_id_type=MESH,
    )


def split_three(value):
    high = value.astype(BF16).astype(F32)
    rest = value - high
    middle = rest.astype(BF16).astype(F32)
    return high, middle, rest - middle


def split_exact(value):
    high = lax.reduce_precision(value, 8, 7)
    middle = lax.reduce_precision(value - high, 8, 7)
    return high, middle, lax.reduce_precision(value - high - middle, 8, 7)


def with_aux(rows, value):
    lane = lax.broadcasted_iota(jnp.int32, rows.shape, 1)
    filled = rows.astype(F32)
    for step, part in enumerate(split_three(value)):
        filled = jnp.where(lane == AUX_LANE + step, part, filled)
    return filled.astype(BF16)


def finish(total, peak, q):
    denominator = total[:, SUM_LANE : SUM_LANE + 1]
    lse = peak + jnp.log(denominator) * (1.0 / LN2)
    return total / denominator, with_aux(q, -lse)


def local_pieces(kv_ref, block, ring):
    count = 1 << (ring - 1)
    start = (block // count) ^ 1
    prefix = SEGMENT_TILES >> ring
    return [(start * count + t, prefix) for t in range(count)]


def send_keys(blocks, all_ref, far_refs, send_sem, recv_sem):
    first_ring = blocks.bit_length()
    direct, passed = [], []
    for step, (ring, place, flip) in enumerate(ring_flips(blocks)):
        far_ref = far_refs[ring - first_ring]
        target = far_ref.at[:, pl.ds(place * blocks, blocks)]
        if flip == 1 or flip % 2 == 0:
            source = all_ref.at[:, :, pl.ds(0, SEGMENT_TILES >> ring)]
            copies, device = direct, sequence_device(flip)
        else:
            source = far_ref.at[:, pl.ds((place - 1) * blocks, blocks)]
            copies, device = passed, sequence_device(1)
        copies.append(remote(source, target, device, send_sem, recv_sem, step))
    return direct, passed


def near_and_far(blocks):
    return [sequence_device(f) for _, _, f in ring_flips(blocks) if f == 1 or f % 2 == 0]


def attend_near_kernel(local_rings, q_ref, kv_ref, bias_ref, all_ref, o_ref, qa_ref, *rest):
    far_refs, (send_sem, recv_sem) = rest[:-2], rest[-2:]
    head, block = pl.program_id(0), pl.program_id(1)
    first = SEGMENT_TILES >> (local_rings + 1)
    blocks = 1 << local_rings

    @pl.when((head == 0) & (block == 0))
    def _():
        greet(near_and_far(blocks))
        direct, _ = send_keys(blocks, all_ref, far_refs, send_sem, recv_sem)
        for copy in direct:
            copy.start()

    @pl.when((head == pl.num_programs(0) - 1) & (block == 0))
    def _():
        direct, passed = send_keys(blocks, all_ref, far_refs, send_sem, recv_sem)
        for copy in direct:
            copy.wait_recv()
        for copy in passed:
            copy.start()

    for level in range(local_rings + 1):
        low, high = class_rows(level)
        size = min(256, high - low)
        for start in range(low, high, size):
            q = q_ref[0, 0, start : start + size, :]
            keys = [(kv_ref[0, block], 0)]
            place = SEGMENT_TILES
            for ring in range(1, level + 1):
                for other, prefix in local_pieces(kv_ref, block, ring):
                    keys.append((kv_ref[0, other, :prefix], place))
                    place += prefix
            scores = [
                dot(q, kv, 1, 1) + bias_ref[0, 0, level : level + 1, at : at + kv.shape[0]]
                for kv, at in keys
            ]
            peak = functools.reduce(
                jnp.maximum, [jnp.max(s, axis=1, keepdims=True) for s in scores]
            )
            total = sum(
                dot(jnp.exp2(s - peak).astype(BF16), kv, 1, 0) for s, (kv, _) in zip(scores, keys)
            )
            out, extended = finish(total, peak, q)
            o_ref[0, 0, start - first : start - first + size, :] = out
            qa_ref[0, 0, start - first : start - first + size, :] = extended

    @pl.when((head == pl.num_programs(0) - 1) & (block == blocks - 1))
    def _():
        direct, passed = send_keys(blocks, all_ref, far_refs, send_sem, recv_sem)
        for copy in direct:
            copy.wait_send()
        for copy in passed:
            copy.wait()


def attend_near(q, kv, bias, collective_id):
    heads, blocks = q.shape[:2]
    local_rings = blocks.bit_length() - 1
    rows = SEGMENT_TILES - (SEGMENT_TILES >> (local_rings + 1))
    spec = pl.BlockSpec((1, 1, rows, LANES), lambda h, k: (h, k, 0, 0))
    pairs = heads * blocks * rows * 1400
    fars = [
        jax.ShapeDtypeStruct((heads, 1 << (ring - 1), SEGMENT_TILES >> ring, LANES), BF16)
        for ring in range(local_rings + 1, LEVELS)
    ]
    copies = len(ring_flips(blocks))
    return pl.pallas_call(
        functools.partial(attend_near_kernel, local_rings),
        grid=(heads, blocks),
        in_specs=[
            pl.BlockSpec((1, 1, SEGMENT_TILES, LANES), lambda h, k: (h, k, 0, 0)),
            pl.BlockSpec((1, blocks, SEGMENT_TILES, LANES), lambda h, k: (h, 0, 0, 0)),
            pl.BlockSpec((1, 1) + bias.shape[2:], lambda h, k: (h, k, 0, 0)),
            pl.BlockSpec(memory_space=pl.ANY),
        ],
        out_specs=[spec, spec] + [pl.BlockSpec(memory_space=pl.ANY)] * len(fars),
        out_shape=[
            jax.ShapeDtypeStruct((heads, blocks, rows, LANES), F32),
            jax.ShapeDtypeStruct((heads, blocks, rows, LANES), BF16),
        ]
        + fars,
        scratch_shapes=[pltpu.SemaphoreType.DMA((copies,)), pltpu.SemaphoreType.DMA((copies,))],
        cost_estimate=pl.CostEstimate(
            flops=pairs * 1024, bytes_accessed=heads * blocks * rows * 1500, transcendentals=pairs
        ),
        compiler_params=pltpu.CompilerParams(
            vmem_limit_bytes=VMEM_LIMIT, collective_id=collective_id, has_side_effects=True
        ),
        name="attend_near",
    )(q, kv, bias, kv)


def far_groups(local_rings):
    groups = []
    for level in range(local_rings + 1, LEVELS):
        low, high = class_rows(level)
        groups.append((level, low, high))
    return sorted(groups, key=lambda group: group[1])


def add_bias(scores, bias_ref, block, at, groups, rows):
    width = scores.shape[1]
    parts = []
    for level, low, high in groups:
        if low < rows:
            parts.append(scores[low:high] + bias_ref[0, block, level : level + 1, at : at + width])
    return parts[0] if len(parts) == 1 else jnp.concatenate(parts, axis=0)


def far_score_list(local_rings, blocks, left_ref, kv_ref, far_ref):
    rows = SEGMENT_TILES >> (local_rings + 1)
    pieces = []
    for block in range(blocks):
        pieces.append((0, block, block, SEGMENT_TILES, rows, 0))
    for block in range(blocks):
        place = SEGMENT_TILES
        for ring in range(1, local_rings + 1):
            for other, prefix in local_pieces(kv_ref, block, ring):
                pieces.append((ring, block, other, prefix, rows, place))
                place += prefix
    for ring in range(local_rings + 1, LEVELS):
        pieces.append((ring, None, None, RING_KEYS, SEGMENT_TILES >> ring, SEGMENT_TILES + (ring - 1) * RING_KEYS))
    return pieces


def far_keys(piece, kv_ref, far_ref, local_rings):
    ring, block, other, prefix, rows, place = piece
    if block is not None:
        return kv_ref[0, other, :prefix]
    return far_ref[ring - local_rings - 1][0]


def far_left(piece, left_ref, blocks):
    ring, block, other, prefix, rows, place = piece
    if block is not None:
        return left_ref[0, block, :rows, :]
    return jnp.concatenate([left_ref[0, one, :rows, :] for one in range(blocks)], axis=0)


def pad_rows(value, rows, fill):
    if value.shape[0] == rows:
        return value
    return jnp.concatenate(
        [value, jnp.full((rows - value.shape[0],) + value.shape[1:], fill, value.dtype)], axis=0
    )


def attend_far_kernel(local_rings, blocks, q_ref, kv_ref, bias_ref, *rest):
    far_ref, (o_ref, qa_ref) = rest[:-2], rest[-2:]
    rows = SEGMENT_TILES >> (local_rings + 1)
    groups = far_groups(local_rings)
    pieces = far_score_list(local_rings, blocks, q_ref, kv_ref, far_ref)
    held = []
    peaks = [None] * blocks
    for piece in pieces:
        ring, block, other, prefix, count, place = piece
        scores = dot(far_left(piece, q_ref, blocks), far_keys(piece, kv_ref, far_ref, local_rings), 1, 1)
        for one in [block] if block is not None else range(blocks):
            part = scores if block is not None else scores[one * count : (one + 1) * count]
            part = add_bias(part, bias_ref, one, place, groups, count)
            held.append((piece, one, part))
            top = pad_rows(jnp.max(part, axis=1, keepdims=True), rows, masked_low)
            peaks[one] = top if peaks[one] is None else jnp.maximum(peaks[one], top)
    totals = [jnp.zeros((rows, LANES), F32)] * blocks
    for piece in pieces:
        weights = [
            (one, jnp.exp2(part - peaks[one][: piece[4]]).astype(BF16))
            for owner, one, part in held
            if owner is piece
        ]
        joined = weights[0][1] if len(weights) == 1 else jnp.concatenate([w for _, w in weights], axis=0)
        product = dot(joined, far_keys(piece, kv_ref, far_ref, local_rings), 1, 0)
        for at, (one, _) in enumerate(weights):
            part = product[at * piece[4] : (at + 1) * piece[4]]
            totals[one] = totals[one] + pad_rows(part, rows, 0.0)
    for block in range(blocks):
        out, extended = finish(totals[block], peaks[block], q_ref[0, block, :rows, :])
        o_ref[0, block] = out
        qa_ref[0, block] = extended


def attend_far(q, kv, far, bias):
    heads, blocks = q.shape[:2]
    local_rings = blocks.bit_length() - 1
    rows = SEGMENT_TILES >> (local_rings + 1)
    whole = lambda shape: pl.BlockSpec((1,) + shape[1:], lambda h: (h,) + (0,) * (len(shape) - 1))
    shape = (heads, blocks, rows, LANES)
    pairs = heads * blocks * rows * 2600
    return pl.pallas_call(
        functools.partial(attend_far_kernel, local_rings, blocks),
        grid=(heads,),
        in_specs=[
            pl.BlockSpec((1, blocks, rows, LANES), lambda h: (h, 0, 0, 0)),
            whole(kv.shape),
            whole(bias.shape),
        ]
        + [whole(one.shape) for one in far],
        out_specs=[whole(shape), whole(shape)],
        out_shape=[jax.ShapeDtypeStruct(shape, F32), jax.ShapeDtypeStruct(shape, BF16)],
        cost_estimate=pl.CostEstimate(
            flops=pairs * 1024, bytes_accessed=heads * 4 * 1024 * 1024, transcendentals=pairs
        ),
        compiler_params=pltpu.CompilerParams(vmem_limit_bytes=VMEM_LIMIT),
        name="attend_far",
    )(q, kv, bias, *far)


def placement(heads):
    table = np.zeros((heads * LANES, heads * HEAD_WIDTH), np.float32)
    for head in range(heads):
        for column in range(HEAD_WIDTH):
            table[head * LANES + HEAD_WIDTH + column, head * HEAD_WIDTH + column] = 1
    return table


def pair_placement(width):
    table = np.zeros((2, width, 2 * width), np.float32)
    column = np.arange(width)
    table[0, column, column] = 1
    table[1, column, width + column] = 1
    return table


def side_by_side(rows, table_ref):
    half = rows.shape[0] // 2
    return dot(rows[:half], table_ref[0], 1, 0) + dot(rows[half:], table_ref[1], 1, 0)


def pack_kernel(heads, row_count, base_ref, far_ref, near_ref, place_ref, out_ref, held_ref):
    piece = row_count // RESIDUES
    halves = SEGMENT_TILES // row_count
    far_rows = far_ref.shape[2]
    for head in range(heads):
        columns = slice(head * LANES, (head + 1) * LANES)
        for slab in range(RESIDUES):
            residue = lax.rem(base_ref[0] + head + ORDER[slab], RESIDUES)
            for half in range(halves):
                start = slab * SLAB + half * piece
                if start < far_rows:
                    value = far_ref[head, 0, start : start + piece, :]
                else:
                    value = near_ref[head, 0, start - far_rows : start - far_rows + piece, :]
                target = pl.ds(pl.multiple_of(half * row_count + residue * piece, piece), piece)
                held_ref[target, columns] = value.astype(BF16)
    for half in range(halves):
        rows = held_ref[half * row_count : (half + 1) * row_count, :]
        out_ref[half] = side_by_side(rows, place_ref).astype(BF16)


def pack_table(heads):
    pairs = pair_placement(heads * HEAD_WIDTH)
    return jnp.asarray(np.stack([placement(heads) @ one for one in pairs]), BF16)


def pack(base, far, near, row_count):
    heads, blocks = far.shape[:2]
    place = pack_table(heads)
    width = heads * HEAD_WIDTH
    halves = SEGMENT_TILES // row_count
    part = lambda shape: pl.BlockSpec((heads, 1) + shape[2:], lambda k, *_: (0, k, 0, 0))
    return pl.pallas_call(
        functools.partial(pack_kernel, heads, row_count),
        grid_spec=pltpu.PrefetchScalarGridSpec(
            num_scalar_prefetch=1,
            grid=(blocks,),
            in_specs=[part(far.shape), part(near.shape), pl.BlockSpec(place.shape, lambda k, *_: (0, 0, 0))],
            out_specs=pl.BlockSpec((halves, row_count // 2, 2 * width), lambda k, *_: (k, 0, 0)),
            scratch_shapes=[pltpu.VMEM((SEGMENT_TILES, heads * LANES), BF16)],
        ),
        out_shape=jax.ShapeDtypeStruct((blocks * halves, row_count // 2, 2 * width), BF16),
        cost_estimate=pl.CostEstimate(
            flops=2 * blocks * SEGMENT_TILES * heads * LANES * width,
            bytes_accessed=blocks * SEGMENT_TILES * heads * LANES * 5,
            transcendentals=0,
        ),
        compiler_params=pltpu.CompilerParams(vmem_limit_bytes=VMEM_LIMIT),
        name="pack",
    )(base, far, near, place)


def unpack_kernel(heads, row_count, base_ref, g_ref, far_ref, near_ref, place_ref, out_ref, held_ref):
    piece = row_count // RESIDUES
    halves = SEGMENT_TILES // row_count
    far_rows = far_ref.shape[2]
    for half in range(halves):
        for side in range(2):
            start = half * row_count + side * (row_count // 2)
            held_ref[start : start + row_count // 2, :] = dot(g_ref[half], place_ref[side], 1, 1)
    for head in range(heads):
        columns = slice(head * LANES, (head + 1) * LANES)
        for slab in range(RESIDUES):
            residue = lax.rem(base_ref[0] + head + ORDER[slab], RESIDUES)
            for half in range(halves):
                start = slab * SLAB + half * piece
                if start < far_rows:
                    value = far_ref[head, 0, start : start + piece, :]
                else:
                    value = near_ref[head, 0, start - far_rows : start - far_rows + piece, :]
                source = pl.ds(pl.multiple_of(half * row_count + residue * piece, piece), piece)
                grad = held_ref[source, columns]
                delta = jnp.sum(grad * value, axis=1, keepdims=True)
                out_ref[head, 0, start : start + piece, :] = with_aux(grad, -delta)


def unpack(base, grad, far, near, row_count):
    heads, blocks = far.shape[:2]
    place = pack_table(heads)
    width = heads * HEAD_WIDTH
    halves = SEGMENT_TILES // row_count
    part = lambda shape: pl.BlockSpec((heads, 1) + shape[2:], lambda k, *_: (0, k, 0, 0))
    shape = (heads, blocks, SEGMENT_TILES, LANES)
    return pl.pallas_call(
        functools.partial(unpack_kernel, heads, row_count),
        grid_spec=pltpu.PrefetchScalarGridSpec(
            num_scalar_prefetch=1,
            grid=(blocks,),
            in_specs=[
                pl.BlockSpec((halves, row_count // 2, 2 * width), lambda k, *_: (k, 0, 0)),
                part(far.shape),
                part(near.shape),
                pl.BlockSpec(place.shape, lambda k, *_: (0, 0, 0)),
            ],
            out_specs=part(shape),
            scratch_shapes=[pltpu.VMEM((SEGMENT_TILES, heads * LANES), F32)],
        ),
        out_shape=jax.ShapeDtypeStruct(shape, BF16),
        cost_estimate=pl.CostEstimate(
            flops=2 * blocks * SEGMENT_TILES * heads * LANES * width,
            bytes_accessed=blocks * SEGMENT_TILES * heads * LANES * 7,
            transcendentals=0,
        ),
        compiler_params=pltpu.CompilerParams(vmem_limit_bytes=VMEM_LIMIT),
        name="unpack",
    )(base, grad, far, near, place)


def returns(blocks):
    first_ring = blocks.bit_length()
    return [max(1, len(ring_members(ring, blocks)) // 2) for ring in range(first_ring, LEVELS)]


def send_back(blocks, dfar_refs, take_refs, sum_refs, back_refs, send_sem, recv_sem):
    first_ring = blocks.bit_length()
    crossing, sums, last = [], [], []
    for step, (ring, place, flip) in enumerate(ring_flips(blocks)):
        at = ring - first_ring
        rows = blocks * (SEGMENT_TILES >> ring)
        source = dfar_refs[at].at[:, pl.ds(place * rows, rows)]
        if flip == 1:
            target = back_refs[at].at[0]
            crossing.append(remote(source, target, sequence_device(1), send_sem, recv_sem, step))
        elif flip % 2:
            target = take_refs[at].at[place // 2]
            crossing.append(remote(source, target, sequence_device(1), send_sem, recv_sem, step))
        else:
            summed = sum_refs[at].at[place // 2]
            sums.append((source, take_refs[at].at[place // 2], summed))
            target = back_refs[at].at[place // 2]
            last.append(remote(summed, target, sequence_device(flip), send_sem, recv_sem, step))
    return crossing, sums, last


def back_near_kernel(local_rings, qa_ref, do_ref, kv_ref, bias_ref, *rest):
    fars = LEVELS - 1 - local_rings
    dfar_refs, (dq_ref, dkv_ref) = rest[:fars], rest[fars : fars + 2]
    back_refs, rest = rest[fars + 2 : 2 * fars + 2], rest[2 * fars + 2 :]
    take_refs, sum_refs, sems = (None,) + rest[: fars - 1], (None,) + rest[fars - 1 : -2], rest[-2:]
    head, block = pl.program_id(0), pl.program_id(1)
    first = SEGMENT_TILES >> (local_rings + 1)
    blocks = 1 << local_rings
    copies = lambda: send_back(blocks, dfar_refs, take_refs, sum_refs, back_refs, *sems)

    @pl.when((head == 0) & (block == 0))
    def _():
        greet(near_and_far(blocks))
        for copy in copies()[0]:
            copy.start()

    @pl.when((head == 1) & (block == 0))
    def _():
        crossing, sums, last = copies()
        for copy in crossing:
            copy.wait_recv()
        for own, taken, summed in sums:
            summed[...] = (own[...].astype(F32) + taken[...].astype(F32)).astype(BF16)
        for copy in last:
            copy.start()

    @pl.when(block == 0)
    def _():
        dkv_ref[...] = jnp.zeros_like(dkv_ref)

    for level in range(local_rings + 1):
        low, high = class_rows(level)
        size = min(256, high - low)
        for start in range(low, high, size):
            here = slice(start - first, start - first + size)
            q = qa_ref[0, 0, here, :]
            grad = do_ref[0, 0, start : start + size, :]
            q_turned, grad_turned = q.T, grad.T
            keys = [(block, SEGMENT_TILES, 0)]
            place = SEGMENT_TILES
            for ring in range(1, level + 1):
                for other, prefix in local_pieces(kv_ref, block, ring):
                    keys.append((other, prefix, place))
                    place += prefix
            dq = jnp.zeros((size, LANES), F32)
            for other, prefix, at in keys:
                kv = kv_ref[0, other, :prefix]
                scores = dot(q, kv, 1, 1) + bias_ref[0, 0, level : level + 1, at : at + prefix]
                weights = jnp.exp2(scores)
                grads = (weights * dot(grad, kv, 1, 1)).astype(BF16)
                dq = dq + dot(grads, kv, 1, 0)
                dkv_ref[0, other, :, :prefix] += dot(q_turned, grads, 1, 0) + dot(
                    grad_turned, weights.astype(BF16), 1, 0
                )
            dq_ref[0, 0, here, :] = dq

    @pl.when((head == pl.num_programs(0) - 1) & (block == blocks - 1))
    def _():
        crossing, _, last = copies()
        for copy in crossing:
            copy.wait_send()
        for copy in last:
            copy.wait()


def back_near(qa, do, kv, bias, dfar, collective_id):
    heads, blocks = kv.shape[:2]
    local_rings = blocks.bit_length() - 1
    rows = qa.shape[2]
    spec = pl.BlockSpec((1, 1, rows, LANES), lambda h, k: (h, k, 0, 0))
    pairs = heads * blocks * rows * 1400
    anywhere = pl.BlockSpec(memory_space=pl.ANY)
    backs = [
        jax.ShapeDtypeStruct((count, heads, blocks * (SEGMENT_TILES >> ring), LANES), BF16)
        for ring, count in zip(range(local_rings + 1, LEVELS), returns(blocks))
    ]
    copies = len(ring_flips(blocks))
    return pl.pallas_call(
        functools.partial(back_near_kernel, local_rings),
        grid=(heads, blocks),
        in_specs=[
            spec,
            pl.BlockSpec((1, 1, SEGMENT_TILES, LANES), lambda h, k: (h, k, 0, 0)),
            pl.BlockSpec((1, blocks, SEGMENT_TILES, LANES), lambda h, k: (h, 0, 0, 0)),
            pl.BlockSpec((1, 1) + bias.shape[2:], lambda h, k: (h, k, 0, 0)),
        ]
        + [pl.BlockSpec(one.shape, lambda h, k: (0, 0, 0)) for one in dfar],
        out_specs=[spec, pl.BlockSpec((1, blocks, LANES, SEGMENT_TILES), lambda h, k: (h, 0, 0, 0))]
        + [anywhere] * len(backs),
        out_shape=[
            jax.ShapeDtypeStruct((heads, blocks, rows, LANES), F32),
            jax.ShapeDtypeStruct((heads, blocks, LANES, SEGMENT_TILES), F32),
        ]
        + backs,
        scratch_shapes=[pltpu.VMEM(one.shape, BF16) for one in backs[1:] + backs[1:]]
        + [pltpu.SemaphoreType.DMA((copies,)), pltpu.SemaphoreType.DMA((copies,))],
        cost_estimate=pl.CostEstimate(
            flops=pairs * 2560, bytes_accessed=heads * blocks * rows * 2500, transcendentals=pairs
        ),
        compiler_params=pltpu.CompilerParams(
            vmem_limit_bytes=VMEM_LIMIT, collective_id=collective_id, has_side_effects=True
        ),
        name="back_near",
    )(qa, do, kv, bias, *dfar)


def back_far_kernel(local_rings, blocks, qa_ref, do_ref, kv_ref, bias_ref, *rest):
    fars = LEVELS - 1 - local_rings
    far_ref, (dq_ref, dkv_ref), dfar_ref = rest[:fars], rest[fars : fars + 2], rest[fars + 2 :]
    rows = SEGMENT_TILES >> (local_rings + 1)
    groups = far_groups(local_rings)
    dq_ref[...] = jnp.zeros_like(dq_ref)
    for piece in far_score_list(local_rings, blocks, qa_ref, kv_ref, far_ref):
        ring, block, other, prefix, count, place = piece
        q = far_left(piece, qa_ref, blocks)
        grad = far_left(piece, do_ref, blocks)
        kv = far_keys(piece, kv_ref, far_ref, local_rings)
        raw = dot(q, kv, 1, 1)
        owners = [block] if block is not None else range(blocks)
        parts = [
            add_bias(raw[at * count : (at + 1) * count], bias_ref, one, place, groups, count)
            for at, one in enumerate(owners)
        ]
        scores = parts[0] if len(parts) == 1 else jnp.concatenate(parts, axis=0)
        weights = jnp.exp2(scores)
        grads = (weights * dot(grad, kv, 1, 1)).astype(BF16)
        dq = dot(grads, kv, 1, 0)
        for at, one in enumerate(owners):
            dq_ref[0, one, :count, :] += dq[at * count : (at + 1) * count]
        dkv = dot(q.T, grads, 1, 0) + dot(grad.T, weights.astype(BF16), 1, 0)
        if block is None:
            dfar_ref[ring - local_rings - 1][0] = dkv.T.astype(BF16)
        elif ring == 0:
            dkv_ref[0, other] = dkv
        else:
            dkv_ref[0, other, :, :prefix] += dkv


def back_far(qa, do, kv, far, bias):
    heads, blocks = kv.shape[:2]
    local_rings = blocks.bit_length() - 1
    rows = SEGMENT_TILES >> (local_rings + 1)
    whole = lambda shape: pl.BlockSpec((1,) + shape[1:], lambda h: (h,) + (0,) * (len(shape) - 1))
    pairs = heads * blocks * rows * 2600
    turned = (heads, blocks, LANES, SEGMENT_TILES)
    return pl.pallas_call(
        functools.partial(back_far_kernel, local_rings, blocks),
        grid=(heads,),
        in_specs=[
            whole(qa.shape),
            pl.BlockSpec((1, blocks, rows, LANES), lambda h: (h, 0, 0, 0)),
            whole(kv.shape),
            whole(bias.shape),
        ]
        + [whole(one.shape) for one in far],
        out_specs=[whole(qa.shape), whole(turned)] + [whole(one.shape) for one in far],
        out_shape=[
            jax.ShapeDtypeStruct(qa.shape, F32),
            jax.ShapeDtypeStruct(turned, F32),
        ]
        + [jax.ShapeDtypeStruct(one.shape, BF16) for one in far],
        cost_estimate=pl.CostEstimate(
            flops=pairs * 2560, bytes_accessed=heads * 6 * 1024 * 1024, transcendentals=pairs
        ),
        compiler_params=pltpu.CompilerParams(vmem_limit_bytes=VMEM_LIMIT),
        name="back_far",
    )(qa, do, kv, bias, *far)


def narrow(heads):
    local_width = heads * HEAD_WIDTH
    table = np.zeros((heads, 2 * LANES, 3 * local_width), np.float32)
    column = np.arange(HEAD_WIDTH)
    for head in range(heads):
        start = head * HEAD_WIDTH + column
        table[head, column, start] = 1
        table[head, LANES + column, local_width + start] = 1
        table[head, LANES + HEAD_WIDTH + column, 2 * local_width + start] = 1
    return table.reshape(heads * 2 * LANES, 3 * local_width)


def collect_kernel(heads, row_count, counts, score_scale, base_ref, *refs):
    dq_far_ref, dq_near_ref, one_ref, two_ref = refs[:4]
    returned = refs[4 : 4 + len(counts)]
    place_ref, out_ref, held_ref, wide_ref = refs[4 + len(counts) :]
    piece = row_count // RESIDUES
    halves = SEGMENT_TILES // row_count
    far_rows = dq_far_ref.shape[2]
    for head in range(heads):
        held_ref[...] = (one_ref[head, 0] + two_ref[head, 0]).T
        for back_ref, count in zip(returned, counts):
            held_ref[:count, :] += back_ref[head, 0].astype(F32)
        lane = lax.broadcasted_iota(jnp.int32, (piece, LANES), 1)
        factor = jnp.where(lane < HEAD_WIDTH, LN2, jnp.where(lane < SUM_LANE, 1.0, 0.0))
        q_factor = jnp.where(lane < HEAD_WIDTH, score_scale, 0.0)
        for slab in range(RESIDUES):
            residue = lax.rem(base_ref[0] + head + ORDER[slab], RESIDUES)
            for half in range(halves):
                start = slab * SLAB + half * piece
                if start < far_rows:
                    value = dq_far_ref[head, 0, start : start + piece, :]
                else:
                    value = dq_near_ref[head, 0, start - far_rows : start - far_rows + piece, :]
                target = pl.ds(pl.multiple_of(half * row_count + residue * piece, piece), piece)
                at = head * 2 * LANES
                wide_ref[target, at : at + LANES] = (value * q_factor).astype(BF16)
                wide_ref[target, at + LANES : at + 2 * LANES] = (
                    held_ref[start : start + piece, :] * factor
                ).astype(BF16)
    out_ref[...] = dot(wide_ref[...], place_ref[...], 1, 0).astype(BF16)


def collect(base, dq_far, dq_near, dkv_one, dkv_two, returned, row_count, score_scale):
    heads, blocks = dq_far.shape[:2]
    counts = tuple(one.shape[2] for one in returned)
    part = lambda shape: pl.BlockSpec((heads, 1) + shape[2:], lambda k, *_: (0, k, 0, 0))
    arrays = (dq_far, dq_near, dkv_one, dkv_two) + tuple(returned)
    place = jnp.asarray(narrow(heads), BF16)
    wide, width = place.shape
    return pl.pallas_call(
        functools.partial(collect_kernel, heads, row_count, counts, score_scale),
        grid_spec=pltpu.PrefetchScalarGridSpec(
            num_scalar_prefetch=1,
            grid=(blocks,),
            in_specs=[part(one.shape) for one in arrays]
            + [pl.BlockSpec(place.shape, lambda k, *_: (0, 0))],
            out_specs=pl.BlockSpec((SEGMENT_TILES, width), lambda k, *_: (k, 0)),
            scratch_shapes=[
                pltpu.VMEM((SEGMENT_TILES, LANES), F32),
                pltpu.VMEM((SEGMENT_TILES, wide), BF16),
            ],
        ),
        out_shape=jax.ShapeDtypeStruct((blocks * SEGMENT_TILES, width), BF16),
        cost_estimate=pl.CostEstimate(
            flops=2 * blocks * SEGMENT_TILES * wide * width,
            bytes_accessed=blocks * SEGMENT_TILES * wide * 10,
            transcendentals=0,
        ),
        compiler_params=pltpu.CompilerParams(vmem_limit_bytes=VMEM_LIMIT),
        name="collect",
    )(base, *arrays, place)


def exchange_kernel(count, x_ref, out_ref, send_sem, recv_sem, local_sem):
    rank = lax.axis_index("head")
    greet([{"head": partner(rank, flip)} for flip in range(1, count)])
    keep = pltpu.make_async_copy(x_ref.at[rank], out_ref.at[0], local_sem)
    keep.start()
    copies = []
    for flip in range(1, count):
        to = partner(rank, flip)
        copies.append(
            pltpu.make_async_remote_copy(
                src_ref=x_ref.at[to],
                dst_ref=out_ref.at[flip],
                send_sem=send_sem.at[flip - 1],
                recv_sem=recv_sem.at[flip - 1],
                device_id={"head": to},
                device_id_type=MESH,
            )
        )
        copies[-1].start()
    for copy in copies:
        copy.wait()
    keep.wait()


def exchange_back_kernel(count, x_ref, out_ref, send_sem, recv_sem, local_sem):
    rank = lax.axis_index("head")
    greet([{"head": partner(rank, flip)} for flip in range(1, count)])
    keep = pltpu.make_async_copy(x_ref.at[0], out_ref.at[rank], local_sem)
    keep.start()
    copies = []
    for flip in range(1, count):
        copies.append(
            pltpu.make_async_remote_copy(
                src_ref=x_ref.at[flip],
                dst_ref=out_ref.at[rank],
                send_sem=send_sem.at[flip - 1],
                recv_sem=recv_sem.at[flip - 1],
                device_id={"head": partner(rank, flip)},
                device_id_type=MESH,
            )
        )
        copies[-1].start()
    for copy in copies:
        copy.wait()
    keep.wait()


def exchange_rows(parts, collective_id):
    return exchange_call(exchange_kernel, parts, collective_id)


def exchange_back(parts, collective_id):
    return exchange_call(exchange_back_kernel, parts, collective_id)


def exchange_call(kernel, parts, collective_id):
    count = parts.shape[0]
    return pl.pallas_call(
        functools.partial(kernel, count),
        in_specs=[pl.BlockSpec(memory_space=pltpu.VMEM)],
        out_specs=pl.BlockSpec(memory_space=pltpu.VMEM),
        out_shape=jax.ShapeDtypeStruct(parts.shape, parts.dtype),
        scratch_shapes=[
            pltpu.SemaphoreType.DMA((count - 1,)),
            pltpu.SemaphoreType.DMA((count - 1,)),
            pltpu.SemaphoreType.DMA,
        ],
        compiler_params=pltpu.CompilerParams(
            collective_id=collective_id, has_side_effects=True, vmem_limit_bytes=VMEM_LIMIT
        ),
        name="exchange_rows",
    )(parts)


def gather_kernel(x_ref, out_ref, send_sem, recv_sem, local_sem):
    rank = lax.axis_index("head")
    side, across = partner(rank, 1), partner(rank, 2)
    greet([{"head": side}, {"head": across}])
    half = x_ref.shape[0] // 2
    first, second = pl.ds(0, half), pl.ds(half, half)
    keep = pltpu.make_async_copy(x_ref, out_ref.at[rank], local_sem)
    keep.start()

    def send(step, source, owner, part, to):
        copy = pltpu.make_async_remote_copy(
            src_ref=source.at[part],
            dst_ref=out_ref.at[owner, part],
            send_sem=send_sem.at[step],
            recv_sem=recv_sem.at[step],
            device_id={"head": to},
            device_id_type=MESH,
        )
        copy.start()
        return copy

    copies = [
        send(0, x_ref, rank, first, side),
        send(1, x_ref, rank, second, across),
        send(2, x_ref, rank, second, side),
        send(3, x_ref, rank, first, across),
    ]
    copies[0].wait_recv()
    copies.append(send(4, out_ref.at[side], side, first, across))
    copies[1].wait_recv()
    copies.append(send(5, out_ref.at[across], across, second, side))
    for copy in copies[2:]:
        copy.wait_recv()
    for copy in copies:
        copy.wait_send()
    keep.wait()


def gather_rows(rows, collective_id):
    count, width = rows.shape
    return pl.pallas_call(
        gather_kernel,
        in_specs=[pl.BlockSpec(memory_space=pltpu.VMEM)],
        out_specs=pl.BlockSpec(memory_space=pltpu.VMEM),
        out_shape=jax.ShapeDtypeStruct((4, count, width), rows.dtype),
        scratch_shapes=[
            pltpu.SemaphoreType.DMA((6,)),
            pltpu.SemaphoreType.DMA((6,)),
            pltpu.SemaphoreType.DMA,
        ],
        compiler_params=pltpu.CompilerParams(
            collective_id=collective_id, has_side_effects=True, vmem_limit_bytes=VMEM_LIMIT
        ),
        name="gather_rows",
    )(rows).reshape(4 * count, width)


def as_two(value):
    high = value.astype(BF16)
    return high, (value - high.astype(F32)).astype(BF16)


class LineSum:
    def __init__(self, core, send_sem, recv_sem, first_step):
        pair = lax.axis_index("pair")
        low, high = lax.rem(pair, 2), lax.div(pair, 2)
        self.end, self.middle = low == high, low != high
        self.near, self.across = {"pair": partner(pair, 1)}, {"pair": partner(pair, 3)}
        self.other_core = {"core": 1 - core}
        self.sems, self.step, self.pieces = (send_sem, recv_sem), first_step, []

    def add_piece(self, own, taken, swapped):
        step = self.step + 4 * len(self.pieces)
        self.pieces.append(
            {
                "own": own,
                "taken": taken,
                "swapped": swapped,
                "in": remote(own, taken, self.near, *self.sems, step),
                "swap": remote(own, swapped, self.across, *self.sems, step + 1),
                "back": remote(own, swapped, self.near, *self.sems, step + 2),
                "core": remote(own, own, self.other_core, *self.sems, step + 3),
            }
        )

    def begin(self, k):
        @pl.when(self.end)
        def _():
            self.pieces[k]["in"].start()

    def add(self, k, extra):
        own = self.pieces[k]["own"]
        own[...] = (own[...].astype(F32) + extra[...].astype(F32)).astype(BF16)

    def swap(self, k):
        @pl.when(self.middle)
        def _():
            self.pieces[k]["in"].wait_recv()
            self.add(k, self.pieces[k]["taken"])
            self.pieces[k]["swap"].start()

    def finish(self, k):
        @pl.when(self.middle)
        def _():
            self.pieces[k]["swap"].wait()
            self.add(k, self.pieces[k]["swapped"])
            self.pieces[k]["back"].start()
            self.pieces[k]["core"].start()

    def arrive(self, k):
        @pl.when(self.end)
        def _():
            self.pieces[k]["in"].wait_send()
            self.pieces[k]["back"].wait_recv()
            self.pieces[k]["own"][...] = self.pieces[k]["swapped"][...]
            self.pieces[k]["core"].start()

    def close(self):
        for piece in self.pieces:
            piece["core"].wait()

            @pl.when(self.middle)
            def _():
                piece["back"].wait_send()


STEPS = 16
RED_PIECES = 8
DW_PIECES = 4


def finale_kernel(
    proj_ref,
    x_ref,
    w_ref,
    small_ref,
    gain_ref,
    shift_ref,
    hat_ref,
    inv_ref,
    res_ref,
    reduced_ref,
    grad_ref,
    weight_ref,
    total_ref,
    column_ref,
    merged_ref,
    out_buf,
    own_buf,
    side_buf,
    across_buf,
    corner_buf,
    dw_buf,
    dw_send,
    dw_recv,
    dw_all,
    dw_take,
    dw_swap,
    red_buf,
    red_take,
    red_swap,
    small_buf,
    small_recv,
    both_buf,
    both_recv,
    send_sem,
    recv_sem,
):
    rank, pair, core = lax.axis_index("head"), lax.axis_index("pair"), lax.axis_index("core")
    side, across, corner = partner(rank, 1), partner(rank, 2), partner(rank, 3)
    other_core = {"core": 1 - core}
    pairs = [{"pair": partner(pair, flip)} for flip in (1, 2, 3)]
    heads = [{"head": side}, {"head": across}, {"head": corner}]
    greet(heads + pairs + [other_core])
    rows = hat_ref.shape[0]
    half = rows // 2
    first, second = pl.ds(0, half), pl.ds(half, half)
    started = []

    def send(source, target, device):
        copy = remote(source, target, device, send_sem, recv_sem, len(started))
        copy.start()
        started.append(copy)
        return copy

    def share(member):
        piece = proj_ref[pl.ds(pl.multiple_of(member * rows, rows), rows), :]
        return dot(piece, w_ref[...], 1, 1)

    line = LineSum(core, send_sem, recv_sem, STEPS)
    red_buf[core] = reduced_ref[...]
    slim = red_take.shape[1]
    for k in range(RED_PIECES):
        line.add_piece(red_buf.at[core, pl.ds(k * slim, slim)], red_take.at[k], red_swap.at[k])
    thin = dw_take.shape[1]
    for k in range(DW_PIECES):
        line.add_piece(dw_all.at[core, pl.ds(k * thin, thin)], dw_take.at[k], dw_swap.at[k])
    every = RED_PIECES + DW_PIECES
    for k in range(RED_PIECES):
        line.begin(k)

    out_buf[2] = share(corner).astype(BF16)
    via_side = send(out_buf.at[2, first], corner_buf.at[0], heads[0])
    via_across = send(out_buf.at[2, second], corner_buf.at[1], heads[1])
    out_buf[0] = share(side).astype(BF16)
    side_first = send(out_buf.at[0, first], side_buf.at[first], heads[0])
    out_buf[1] = share(across).astype(BF16)
    across_second = send(out_buf.at[1, second], across_buf.at[second], heads[1])

    dw_buf[...] = dot(x_ref[...], proj_ref[...], 0, 0)
    depth = dw_send.shape[0]
    dw_send[...] = dw_buf[pl.ds(pl.multiple_of((1 - core) * depth, depth), depth), :].astype(BF16)
    halves = send(dw_send, dw_recv, other_core)
    line.swap(0)
    line.swap(1)
    columns = dot(jnp.ones((8, proj_ref.shape[0]), BF16), proj_ref[...], 1, 0)
    shift_sum = sum(dot(part, w_ref[...], 1, 1) for part in as_two(columns))
    ones = jnp.ones((8, w_ref.shape[1]), BF16)
    product = w_ref[...].astype(F32) * dw_buf[...]
    gain_sum = sum(dot(ones, part, 1, 1) for part in as_two(product))
    gain_sum = (gain_sum - shift_ref[...] * shift_sum) / gain_ref[...]
    index = lax.broadcasted_iota(jnp.int32, gain_sum.shape, 0)
    small_buf[...] = jnp.where(index == 4, gain_sum, jnp.where(index == 5, shift_sum, small_ref[...]))
    small = [send(small_buf, small_recv.at[step], heads[step]) for step in range(3)]
    halves.wait_recv()
    dw_all[core] = (
        dw_buf[pl.ds(pl.multiple_of(core * depth, depth), depth), :] + dw_recv[...].astype(F32)
    ).astype(BF16)
    for k in range(RED_PIECES, every):
        line.begin(k)
    line.swap(2)
    line.finish(0)
    own_buf[...] = share(rank)
    line.swap(3)
    line.finish(1)

    via_side.wait_recv()
    out_buf[1, first, :] = (out_buf[1, first, :].astype(F32) + corner_buf[0].astype(F32)).astype(BF16)
    across_first = send(out_buf.at[1, first], across_buf.at[first], heads[1])
    via_across.wait_recv()
    out_buf[0, second, :] = (
        out_buf[0, second, :].astype(F32) + corner_buf[1].astype(F32)
    ).astype(BF16)
    side_second = send(out_buf.at[0, second], side_buf.at[second], heads[0])

    line.swap(4)
    line.finish(2)
    for copy in small:
        copy.wait_recv()
    both_buf[0, :8, :] = (small_buf[...] + small_recv[0]) + (small_recv[1] + small_recv[2])
    wide = columns.shape[1]
    both_buf[0, 8:, :] = jnp.zeros_like(both_buf[0, 8:, :])
    both_buf[0, 8:, :wide] = columns
    small_core = send(both_buf.at[0], both_recv.at[0], other_core)
    line.swap(5)
    line.finish(3)
    small_core.wait_recv()
    both_buf[1] = both_buf[0] + both_recv[0]
    small_pairs = [
        send(both_buf.at[1], both_recv.at[1 + step], device) for step, device in enumerate(pairs)
    ]
    for k in range(6, every):
        line.swap(k)
        line.finish(k - 2)
        line.arrive(k - 6)
    line.finish(every - 2)
    line.finish(every - 1)
    for copy in small_pairs:
        copy.wait_recv()
    by_pair = [both_buf[1], both_recv[1], both_recv[2], both_recv[3]]
    total = (by_pair[0] + by_pair[1]) + (by_pair[2] + by_pair[3])
    total_ref[...] = total[:8]
    column_ref[...] = total[8:, :wide]

    for copy in (side_first, side_second, across_first, across_second):
        copy.wait_recv()
    grad = own_buf[...] + side_buf[...].astype(F32) + across_buf[...].astype(F32)
    scaled = grad * gain_ref[...]
    hat = hat_ref[...]
    own_buf[...] = res_ref[...] + inv_ref[...] * (
        scaled
        - jnp.mean(scaled, axis=1, keepdims=True)
        - hat * jnp.mean(scaled * hat, axis=1, keepdims=True)
    )
    group, width = rows // RESIDUES, hat.shape[1]
    for residue in range(RESIDUES):
        grad_ref[:, residue * width : (residue + 1) * width] = own_buf[
            residue * group : (residue + 1) * group, :
        ]
    for k in range(every - 6, every):
        line.arrive(k)
    line.close()
    weight_ref[...] = dw_all[...].reshape(weight_ref.shape)
    merged_ref[...] = red_buf[...]
    for copy in started:
        copy.wait_send()


def finale(proj, rows, weight, small, gain, shift, hat, inverse, residual, reduced, collective_id):
    count, width = hat.shape
    columns = proj.shape[1]
    depth = width // 2
    many = reduced.shape[0]
    steps = STEPS + 4 * (RED_PIECES + DW_PIECES)
    vmem = pl.BlockSpec(memory_space=pltpu.VMEM)
    return pl.pallas_call(
        finale_kernel,
        in_specs=[vmem] * 10,
        out_specs=[vmem] * 5,
        out_shape=[
            jax.ShapeDtypeStruct((count // RESIDUES, RESIDUES * width), F32),
            jax.ShapeDtypeStruct((width, columns), BF16),
            jax.ShapeDtypeStruct((8, width), F32),
            jax.ShapeDtypeStruct((8, columns), F32),
            jax.ShapeDtypeStruct((2, many, width), BF16),
        ],
        scratch_shapes=[
            pltpu.VMEM((3, count, width), BF16),
            pltpu.VMEM((count, width), F32),
            pltpu.VMEM((count, width), BF16),
            pltpu.VMEM((count, width), BF16),
            pltpu.VMEM((2, count // 2, width), BF16),
            pltpu.VMEM((width, columns), F32),
            pltpu.VMEM((depth, columns), BF16),
            pltpu.VMEM((depth, columns), BF16),
            pltpu.VMEM((2, depth, columns), BF16),
            pltpu.VMEM((DW_PIECES, depth // DW_PIECES, columns), BF16),
            pltpu.VMEM((DW_PIECES, depth // DW_PIECES, columns), BF16),
            pltpu.VMEM((2, many, width), BF16),
            pltpu.VMEM((RED_PIECES, many // RED_PIECES, width), BF16),
            pltpu.VMEM((RED_PIECES, many // RED_PIECES, width), BF16),
            pltpu.VMEM((8, width), F32),
            pltpu.VMEM((3, 8, width), F32),
            pltpu.VMEM((2, 16, width), F32),
            pltpu.VMEM((4, 16, width), F32),
            pltpu.SemaphoreType.DMA((steps,)),
            pltpu.SemaphoreType.DMA((steps,)),
        ],
        cost_estimate=pl.CostEstimate(
            flops=4 * proj.shape[0] * width * columns, bytes_accessed=12_000_000, transcendentals=0
        ),
        compiler_params=pltpu.CompilerParams(
            collective_id=collective_id, has_side_effects=True, vmem_limit_bytes=VMEM_LIMIT
        ),
        name="finale",
    )(proj, rows, weight, small, gain, shift, hat, inverse, residual, reduced)


def mid_kernel(
    count,
    attn_ref,
    features_ref,
    cotangent_ref,
    out_mine_ref,
    out_other_ref,
    up_mine_ref,
    down_mine_ref,
    up_other_ref,
    down_other_ref,
    up_bias_ref,
    rows_ref,
    table_ref,
    result_ref,
    merged_ref,
    back_ref,
    grad_ref,
    small_ref,
    residual_buf,
    hat_buf,
    inverse_buf,
    normed_buf,
    total_buf,
    grad_buf,
    up_buf,
    down_buf,
    attn_buf,
    out_buf,
    give_buf,
    take_buf,
    send_sem,
    recv_sem,
):
    step = pl.program_id(0)
    rank, core = lax.axis_index("head"), lax.axis_index("core")
    local_width = table_ref.shape[1]
    slim = local_width // 2
    out_bias, mlp_gain, mlp_shift, down_bias = [rows_ref[k : k + 1, :] for k in range(4)]
    other_core = {"core": 1 - core}
    width = features_ref.shape[1]
    hidden_width = up_buf.shape[1]
    up_rows = width // 2 * hidden_width // width
    down_rows = hidden_width // 2
    body = up_rows + down_rows
    tail = pl.ds(body, slim)

    def piece(k):
        part = pl.ds(0, body)
        return remote(give_buf.at[k, part], take_buf.at[k, part], other_core, send_sem, recv_sem, k)

    def last_piece(k):
        return remote(
            give_buf.at[k, tail], take_buf.at[k, tail], other_core, send_sem, recv_sem, count + k
        )

    def add_taken(k, rows):
        merged_ref[k, rows, :] = (
            merged_ref[k, rows, :].astype(F32) + take_buf[k, rows, :].astype(F32)
        ).astype(BF16)

    half_of = lambda ref, place: pl.ds(
        pl.multiple_of(place * (ref.shape[0] // 2), ref.shape[0] // 2), ref.shape[0] // 2
    )

    @pl.when(step == 0)
    def _():
        greet([other_core])
        half = attn_ref.shape[1]
        total = features_ref[...].astype(F32) + out_bias
        for part in range(count):
            owner = partner(rank, part)
            for side in range(2):
                attn_buf[part, side * half : (side + 1) * half, :] = dot(
                    attn_ref[part], table_ref[side], 1, 1
                ).astype(BF16)
            for ref, place in ((out_mine_ref, core), (out_other_ref, 1 - core)):
                out_buf[part, pl.ds(pl.multiple_of(place * slim, slim), slim), :] = ref[owner]
            total = total + dot(attn_buf[part], out_buf[part], 1, 0)
        residual_buf[...] = total
        center = total - jnp.mean(total, axis=1, keepdims=True)
        inverse = lax.rsqrt(jnp.mean(center * center, axis=1, keepdims=True) + epsilon)
        hat = center * inverse
        hat_buf[...] = hat
        inverse_buf[...] = jnp.broadcast_to(inverse, inverse_buf.shape)
        normed_buf[...] = (hat * mlp_gain + mlp_shift).astype(BF16)
        total_buf[...] = jnp.zeros_like(total_buf)
        grad_buf[...] = jnp.zeros_like(grad_buf)

    for up_ref, down_ref, place in (
        (up_mine_ref, down_mine_ref, core),
        (up_other_ref, down_other_ref, 1 - core),
    ):
        up_buf[half_of(up_buf, place), :] = up_ref[0]
        down_buf[half_of(down_buf, place), :] = down_ref[0]
    normed, cotangent = normed_buf[...], cotangent_ref[...]
    value = dot(normed, up_buf[...], 1, 0) + up_bias_ref[0]
    square = value * value
    factor = math.sqrt(2.0 / math.pi)
    bent = jnp.tanh(factor * value * (1.0 + 0.044715 * square))
    share = 0.5 * (1.0 + bent)
    hidden = (value * share).astype(BF16)
    slope = share + 0.5 * value * (1.0 - bent * bent) * (factor * (1.0 + 3 * 0.044715 * square))
    total_buf[...] += dot(hidden, down_buf[...], 1, 0)
    grad_pre = (dot(cotangent, down_buf[...], 1, 1) * slope).astype(BF16)
    bias_sum = jnp.sum(grad_pre.astype(F32), axis=0, keepdims=True)
    grad_buf[...] += dot(grad_pre, up_buf[...], 1, 1)
    up_buf[...] = dot(normed, grad_pre, 0, 0).astype(BF16)
    down_buf[...] = dot(hidden, cotangent, 0, 0).astype(BF16)
    shape = (up_rows, width)
    give_buf[step, :up_rows, :] = up_buf[half_of(up_buf, 1 - core), :].reshape(shape)
    give_buf[step, up_rows:body, :] = down_buf[half_of(down_buf, 1 - core), :]
    piece(step).start()
    merged_ref[step, :up_rows, :] = up_buf[half_of(up_buf, core), :].reshape(shape)
    merged_ref[step, up_rows:body, :] = down_buf[half_of(down_buf, core), :]
    merged_ref[step, body + slim :, :] = jnp.zeros_like(merged_ref[0, body + slim :, :])
    merged_ref[step, body + slim :, :hidden_width] = jnp.broadcast_to(
        bias_sum, (TAIL_ROWS, hidden_width)
    ).astype(BF16)

    @pl.when(step > 0)
    def _():
        piece(step - 1).wait()
        add_taken(step - 1, pl.ds(0, body))

    @pl.when(step == count - 1)
    def _():
        cotangent32 = cotangent_ref[...].astype(F32)
        hat = hat_buf[...]
        grad = grad_buf[...]
        scaled = grad * mlp_gain
        inverse = inverse_buf[:, :1]
        full = cotangent32 + inverse * (
            scaled
            - jnp.mean(scaled, axis=1, keepdims=True)
            - hat * jnp.mean(scaled * hat, axis=1, keepdims=True)
        )
        grad_ref[...] = full
        low = full.astype(BF16)
        for part in range(count):
            owner = partner(rank, part)
            grad_out = dot(attn_buf[part], low, 0, 0).astype(BF16)
            down_buf[:local_width, :] = grad_out
            own, others = [
                down_buf[pl.ds(pl.multiple_of(place * slim, slim), slim), :]
                for place in (core, 1 - core)
            ]
            merged_ref[owner, body : body + slim, :] = own
            give_buf[owner, body : body + slim, :] = others
        for k in range(count):
            last_piece(k).start()
        for part in range(count):
            back = dot(low, out_buf[part], 1, 1).astype(BF16)
            back_ref[part] = side_by_side(back, table_ref).astype(BF16)
        result_ref[...] = (residual_buf[...] + total_buf[...] + down_bias).astype(BF16)
        sums = [
            jnp.sum(grad * hat, axis=0, keepdims=True),
            jnp.sum(grad, axis=0, keepdims=True),
            jnp.sum(full, axis=0, keepdims=True),
            jnp.sum(cotangent32, axis=0, keepdims=True),
        ]
        small_ref[...] = jnp.concatenate(sums + [jnp.zeros((4, full.shape[1]), F32)], axis=0)
        piece(step).wait()
        add_taken(step, pl.ds(0, body))
        for k in range(count):
            last_piece(k).wait()
            add_taken(k, tail)


def mid(attn, features, cotangent, outs, ups, downs, up_bias, rows, collective_id):
    count = attn.shape[0]
    row_count, width = features.shape
    local_width = attn.shape[2] // 2
    table = jnp.asarray(pair_placement(local_width), BF16)
    hidden = up_bias.shape[2]
    whole = lambda x: pl.BlockSpec(x.shape, lambda k: (0,) * len(x.shape))
    step = lambda shape: pl.BlockSpec((1,) + shape[1:], lambda k: (k,) + (0,) * (len(shape) - 1))
    out_specs = [
        pl.BlockSpec((count, local_width // 2, width), functools.partial(lambda at, k: (0, at, 0), at))
        for _, at in outs
    ]
    up_specs = [
        pl.BlockSpec((1, width // 2, hidden), functools.partial(lambda at, k: (k, at, 0), at))
        for _, at in ups
    ]
    down_specs = [
        pl.BlockSpec((1, hidden // 2, width), functools.partial(lambda at, k: (k, at, 0), at))
        for _, at in downs
    ]
    merged = hidden + local_width // 2 + TAIL_ROWS
    results = [
        jax.ShapeDtypeStruct((row_count, width), BF16),
        jax.ShapeDtypeStruct((count, merged, width), BF16),
        jax.ShapeDtypeStruct(attn.shape, BF16),
        jax.ShapeDtypeStruct((row_count, width), F32),
        jax.ShapeDtypeStruct((8, width), F32),
    ]
    return pl.pallas_call(
        functools.partial(mid_kernel, count),
        grid=(count,),
        in_specs=[whole(attn), whole(features), whole(cotangent)]
        + out_specs
        + [up_specs[0], down_specs[0], up_specs[1], down_specs[1]]
        + [step(up_bias.shape), whole(rows), whole(table)],
        out_specs=[whole(one) for one in results],
        scratch_shapes=[
            pltpu.VMEM((row_count, width), F32),
            pltpu.VMEM((row_count, width), F32),
            pltpu.VMEM((row_count, LANES), F32),
            pltpu.VMEM((row_count, width), BF16),
            pltpu.VMEM((row_count, width), F32),
            pltpu.VMEM((row_count, width), F32),
            pltpu.VMEM((width, hidden), BF16),
            pltpu.VMEM((hidden, width), BF16),
            pltpu.VMEM((count, row_count, local_width), BF16),
            pltpu.VMEM((count, local_width, width), BF16),
            pltpu.VMEM((count, merged, width), BF16),
            pltpu.VMEM((count, merged, width), BF16),
            pltpu.SemaphoreType.DMA((2 * count,)),
            pltpu.SemaphoreType.DMA((2 * count,)),
        ],
        out_shape=results,
        cost_estimate=pl.CostEstimate(
            flops=12 * row_count * width * hidden * count,
            bytes_accessed=30_000_000,
            transcendentals=row_count * hidden * count,
        ),
        compiler_params=pltpu.CompilerParams(
            vmem_limit_bytes=VMEM_LIMIT, collective_id=collective_id, has_side_effects=True
        ),
        name="mid",
    )(
        attn,
        features,
        cotangent,
        outs[0][0],
        outs[1][0],
        ups[0][0],
        downs[0][0],
        ups[1][0],
        downs[1][0],
        up_bias,
        rows,
        table,
    )


def residue_major(rows):
    count, width = rows.shape
    return rows.reshape(count // RESIDUES, RESIDUES, width).swapaxes(0, 1).reshape(count, width)


def position_major(rows):
    count, width = rows.shape
    return rows.reshape(RESIDUES, count // RESIDUES, width).swapaxes(0, 1).reshape(count, width)


def norm_forward(values, norm_gain, norm_shift):
    center = values - jnp.mean(values, axis=-1, keepdims=True)
    inverse = lax.rsqrt(jnp.mean(center * center, axis=-1, keepdims=True) + epsilon)
    normed = center * inverse
    return (normed * norm_gain + norm_shift, normed, inverse)


def norm_backward(grad_out, normed, inverse, norm_gain):
    scaled = grad_out * norm_gain
    return inverse * (
        scaled
        - jnp.mean(scaled, axis=-1, keepdims=True)
        - normed * jnp.mean(scaled * normed, axis=-1, keepdims=True)
    )


def gelu_tanh(values):
    return jax.nn.gelu(values, approximate=True)


def from_other(x, axis, flip):
    return lax.ppermute(x, axis, [(i, i ^ flip) for i in range(lax.axis_size(axis))])


def per_device(
    tile_features,
    slide_lengths,
    qkv_weight,
    qv_bias,
    out_weight,
    out_bias,
    attn_gain,
    attn_shift,
    mlp_gain,
    mlp_shift,
    up_weight,
    up_bias,
    down_weight,
    down_bias,
    output_cotangent,
):
    row_count = tile_features.shape[2]
    width = tile_features.shape[3]
    local_width = qkv_weight.shape[2]
    heads = local_width // HEAD_WIDTH
    sequence_member = lax.axis_index(SEQ)
    head_rank = lax.axis_index("head")
    head_count = lax.axis_size("head")
    extent = row_count * head_count
    blocks = extent // SEGMENT_TILES
    local_rings = blocks.bit_length() - 1
    score_scale = HEAD_WIDTH ** (-0.5)
    query_scale = score_scale / LN2
    core = lax.axis_index("core")
    base = (head_rank * heads).astype(jnp.int32).reshape(1)

    own_rows = residue_major(tile_features.reshape(row_count, width))
    features = own_rows.astype(F32)
    normed_one, hat_one, inv_one = norm_forward(features, attn_gain, attn_shift)
    normed_one = normed_one.astype(BF16)
    pair_count = lax.axis_size("pair")
    square = head_count == 4 and pair_count == 4
    if head_count == 4:
        gathered_one = gather_rows(normed_one, 0)
    else:
        gathered_one = lax.all_gather(normed_one, "head", axis=0, tiled=True)

    by_head = qkv_weight.reshape(width, 3, heads, HEAD_WIDTH)
    query_weight = jnp.pad(by_head[:, 0], ((0, 0), (0, 0), (0, LANES - HEAD_WIDTH)))
    pair_weight = jnp.pad(
        jnp.concatenate([by_head[:, 1], by_head[:, 2]], axis=-1),
        ((0, 0), (0, 0), (0, LANES - 2 * HEAD_WIDTH)),
    )
    wide = jnp.concatenate([query_weight, pair_weight], axis=-1).reshape(width, heads * 2 * LANES)
    scale_row = np.ones((heads, 2 * LANES), np.float32)
    scale_row[:, :HEAD_WIDTH] = query_scale
    by_head_bias = qv_bias.reshape(2, heads, HEAD_WIDTH)
    ones = np.zeros((heads, LANES - 2 * HEAD_WIDTH), np.float32)
    ones[:, : 1 + AUX_COUNT] = 1.0
    wide_bias = jnp.concatenate(
        [
            by_head_bias[0],
            jnp.zeros((heads, LANES - HEAD_WIDTH), F32),
            jnp.zeros((heads, HEAD_WIDTH), F32),
            by_head_bias[1],
            jnp.asarray(ones),
        ],
        axis=1,
    ).reshape(1, heads * 2 * LANES)
    scale_row = jnp.asarray(scale_row).reshape(1, heads * 2 * LANES)
    bias = key_bias(slide_lengths, sequence_member, head_rank * heads, heads, blocks, row_count)

    hidden_local = up_weight.shape[1]
    bias_rows = jnp.zeros((TAIL_ROWS, width), F32)
    for step, one in enumerate(split_exact(up_bias)):
        bias_rows = bias_rows.at[step, :hidden_local].set(one)
    core_half = lambda x: lax.dynamic_slice_in_dim(x, core * (x.shape[0] // 2), x.shape[0] // 2, 0)
    halves = [core_half(one) for one in (up_weight, down_weight, out_weight)]
    up_rows = width // 2 * hidden_local // width
    halves[0] = halves[0].reshape(up_rows, width)
    mine = jnp.concatenate(halves + [bias_rows.astype(BF16)], axis=0)
    mine = lax.all_gather(mine, "head", axis=0)
    q, kv = project(
        base, gathered_one, wide, jnp.concatenate([wide_bias, scale_row], axis=0), heads, row_count
    )
    o_near, qa_near, *far = attend_near(q, kv, bias, 4)
    far = [one.reshape(heads, RING_KEYS, LANES) for one in far]
    mine, *far = lax.optimization_barrier((mine, *far))
    other = from_other(mine, "core", 1)
    o_far, qa_far = attend_far(q, kv, far, bias)
    packed = pack(base, o_far, o_near, row_count)
    attn_parts = exchange_rows(packed, 1)
    body = up_rows + hidden_local // 2
    tail = body + local_width // 2
    bias_parts = mine[:, tail : tail + 3, :hidden_local].astype(F32)
    up_bias_all = (bias_parts[:, 0] + bias_parts[:, 1]) + bias_parts[:, 2]
    if hidden_local == width:
        slim = local_width // 2
        outs = [(one, body // slim) for one in (mine, other)]
        ups = [(one, 0) for one in (mine, other)]
        downs = [(one, 1) for one in (mine, other)]
    else:
        ups = [
            (one[:, :up_rows].reshape(head_count, width // 2, hidden_local), 0)
            for one in (mine, other)
        ]
        downs = [(one[:, up_rows:body], 0) for one in (mine, other)]
        outs = [(one[:, body:tail], 0) for one in (mine, other)]
    cotangent = residue_major(output_cotangent.reshape(row_count, width))
    rows = jnp.stack([out_bias, mlp_gain, mlp_shift, down_bias])
    output, reduced, back, grad_residual, small = mid(
        attn_parts,
        own_rows,
        cotangent,
        outs,
        ups,
        downs,
        up_bias_all[:, None],
        jnp.pad(rows, ((0, 4), (0, 0))),
        6,
    )
    output = position_major(output).reshape(tile_features.shape)
    grad_parts = exchange_back(back, 2)

    do = unpack(base, grad_parts, o_far, o_near, row_count)
    dq_far, dkv_far, *dfar = back_far(qa_far, do, kv, far, bias)
    dq_near, dkv_near, *backs = back_near(qa_near, do, kv, bias, dfar, 5)
    returned = [
        one[place].reshape(heads, blocks, -1, LANES) for one in backs for place in range(one.shape[0])
    ]

    scatter = lambda x: lax.psum_scatter(x, "head", scatter_dimension=0, tiled=True)

    reduced = scatter(reduced.reshape(-1, width))

    grad_proj = collect(base, dq_far, dq_near, dkv_far, dkv_near, returned, row_count, score_scale)
    qkv_flat = qkv_weight.reshape(width, 3 * local_width)
    if square:
        grad_features, grad_qkv, totals, columns, merged = finale(
            grad_proj,
            gathered_one,
            qkv_flat,
            small,
            attn_gain[None],
            attn_shift[None],
            hat_one,
            inv_one,
            grad_residual,
            reduced,
            3,
        )
        columns = columns[0]
        low_half, high_half = merged[0].astype(F32), merged[1].astype(F32)
    else:
        grad_qkv = dot(gathered_one, grad_proj, 0, 0)
        columns = jnp.sum(grad_proj.astype(F32), axis=0)
        weight32 = qkv_flat.astype(F32)
        shift_sum = jnp.sum(weight32 * columns, axis=1)
        gain_sum = (jnp.sum(weight32 * grad_qkv, axis=1) - attn_shift * shift_sum) / attn_gain
        totals = lax.psum(small.at[4].set(gain_sum).at[5].set(shift_sum), EVERY)
        grad_normed_one = scatter(dot(grad_proj, qkv_flat, 1, 1).astype(BF16)).astype(F32)
        grad_features = grad_residual + norm_backward(grad_normed_one, hat_one, inv_one, attn_gain)
        grad_features = position_major(grad_features)
        grad_qkv = lax.psum(grad_qkv.astype(BF16), SEQ)
        columns = lax.psum(columns, SEQ)
        reduced = lax.psum(reduced, "pair")
        given = from_other(reduced, "core", 1)
        low_half = jnp.where(core == 0, reduced, given).astype(F32)
        high_half = jnp.where(core == 0, given, reduced).astype(F32)
    grad_qkv = grad_qkv.astype(F32).reshape(width, 3, local_width)
    grad_qv = jnp.stack([columns[:local_width], columns[2 * local_width :]])
    norm_totals = jnp.stack([totals[4], totals[5], totals[0], totals[1], totals[2], totals[3]])

    together = lambda a, b: jnp.concatenate([low_half[a:b], high_half[a:b]], axis=0)
    grad_up = jnp.concatenate(
        [one[:up_rows].reshape(width // 2, hidden_local) for one in (low_half, high_half)], axis=0
    )
    grad_down = together(up_rows, body)
    grad_out = together(body, tail)
    grad_up_bias = low_half[tail, :hidden_local] + high_half[tail, :hidden_local]
    return (
        output,
        grad_features.reshape(tile_features.shape),
        grad_qkv,
        grad_qv,
        grad_out,
        norm_totals[4],
        norm_totals[0],
        norm_totals[1],
        norm_totals[2],
        norm_totals[3],
        grad_up,
        grad_up_bias,
        grad_down,
        norm_totals[5],
    )


def solution(mesh):
    in_specs = (
        P(("pair", "core"), "head", None, None),
        P(),
        P(None, None, "head"),
        P(None, "head"),
        P("head", None),
        P(),
        P(),
        P(),
        P(),
        P(),
        P(None, "head"),
        P("head"),
        P("head", None),
        P(),
        P(("pair", "core"), "head", None, None),
    )
    out_specs = (
        P(("pair", "core"), "head", None, None),
        P(("pair", "core"), "head", None, None),
        P(None, None, "head"),
        P(None, "head"),
        P("head", None),
        P(),
        P(),
        P(),
        P(),
        P(),
        P(None, "head"),
        P("head"),
        P("head", None),
        P(),
    )
    split = jax.sharding.Mesh(
        mesh.devices.reshape(mesh.shape["head"], mesh.shape["seq"] // 2, 2), ("head", "pair", "core")
    )
    return jax.shard_map(
        per_device, mesh=split, in_specs=in_specs, out_specs=out_specs, check_vma=False
    )
```
